512 devices in a mesh: seq: 128 (over y_lo, x, z), head: 4 (over y_hi, core).
Axes of the slice: x: 4, y: 8 (y_hi: 2, y_lo: 4; y = y_hi * 4 + y_lo), z: 8, core: 2. Of those that a mesh axis runs over, the one named last changes fastest.
Arguments:
- queries: bfloat16 [32768, 32, 128], P('seq', 'head'), may hold values from -10 to 10
- out_gradient: bfloat16 [32768, 32, 128], P('seq', 'head'), may hold values from -6 to 6
- codebook: bfloat16 [2, 2048, 128], replicated, may hold values from -4 to 4
- code_ids: int32 [4, 2, 32768], P('head', None, 'seq'), may hold values from 0 to 2047
- reach_back: int32 [32768], P('seq'), may hold values from 1 to 768
Outputs:
- codebook_gradient: float32 [2, 2048, 128], P(None, ('seq', 'head'))
The draws below stay inside these ranges and needn't reach their ends.
All inputs are finite; a program needn't handle non-finite values.
Results may differ from the reference program's by a relative error of at most 0.007.
Values may be sent and summed in bfloat16 or wider, within the bound.
A program may use at most 64 MiB of HBM per device.

```python
import math
import jax
import jax.numpy as jnp
from jax import lax

TOK_DEV = 256
HD = 128
CW = 2048
KVH = 4
QH = 32
TOKENS = 32768
SPAN = 768


def code_table(key):
    drawn = jax.random.randint(jax.random.fold_in(key, 12), (KVH, 2, TOKENS), 0, CW, dtype=jnp.int32)
    position = jax.random.randint(jax.random.fold_in(key, 15), (), 0, TOKENS, dtype=jnp.int32)
    return drawn.at[0, 0, position].set(CW - 1).at[0, 1, position].set(0)


def draw_code_ids(key, part):
    shared = code_table(key)
    return shared


def draw_codebook(key, part):
    key = jax.random.fold_in(key, 1)
    lookup = jnp.clip(jax.random.normal(jax.random.fold_in(key, 11), (2, CW, HD), jnp.float32), -4.0, 4.0)
    return lookup.astype(jnp.bfloat16)


def draw_reach_back(key, part):
    key = jax.random.fold_in(key, 4)
    lengths = jax.random.randint(jax.random.fold_in(key, 1), (TOKENS,), 1, SPAN + 1, dtype=jnp.int32)
    position = jax.random.randint(jax.random.fold_in(key, 2), (), 0, TOKENS, dtype=jnp.int32)
    return lengths.at[position].set(SPAN)


def draw_queries(key, part):
    key = jax.random.fold_in(key, 2)
    drawn_draw = jnp.clip(jax.random.normal(key, (TOKENS, QH, HD), jnp.float32), -6.0, 6.0)
    return drawn_draw.astype(jnp.bfloat16)


def shard_levels(own_key, shape, cuts, least, high):
    loudness, own = 1.0, jax.random.fold_in(own_key, 6)
    for dim, parts in cuts:
        draws = jnp.exp(jax.random.uniform(jax.random.fold_in(own, dim), (parts,), jnp.float32, least / len(cuts), high / len(cuts)))
        loudness = loudness * jnp.repeat(draws, shape[dim] // parts).reshape([-1 if axis == dim else 1 for axis in range(len(shape))])
    return loudness


def centred(own_key, dims, spread, most, cuts=(), kind=jnp.bfloat16):
    factor_of = shard_levels(own_key, dims, cuts, -0.22, 0.18) if cuts else 1.0
    values = jax.random.normal(own_key, dims, jnp.float32) * spread * factor_of
    return jnp.minimum(jnp.maximum(values, -most), most).astype(kind)


def setup_inputs(seed: int = 0) -> dict:
    streams_of = jax.random.split(jax.random.key(seed), 6)
    return {
        "queries": draw_queries(jax.random.fold_in(streams_of[5], 71), 0),
        "out_gradient": centred(streams_of[1], (TOKENS, QH, HD), 1.0, 6.0, ((0, 128), (1, 4))),
        "codebook": draw_codebook(jax.random.fold_in(streams_of[5], 71), 0),
        "code_ids": draw_code_ids(jax.random.fold_in(streams_of[5], 71), 0),
        "reach_back": draw_reach_back(jax.random.fold_in(streams_of[5], 71), 0),
    }


def reference(queries, out_gradient, codebook, code_ids, reach_back):
    score_scale = 1.0 / math.sqrt(HD)
    window = SPAN + TOK_DEV
    key_rows = codebook[0][code_ids[:, 0, :]]
    value_rows = codebook[1][code_ids[:, 1, :]]
    padded_keys = jnp.pad(key_rows, ((0, 0), (SPAN, 0), (0, 0))).astype(jnp.float32)
    padded_values = jnp.pad(value_rows, ((0, 0), (SPAN, 0), (0, 0))).astype(jnp.float32)
    query_float = queries.astype(jnp.float32).reshape(TOKENS, KVH, QH // KVH, HD)
    cotangent_float = out_gradient.astype(jnp.float32).reshape(TOKENS, KVH, QH // KVH, HD)

    def window_grads(anchor):
        query_block = lax.dynamic_slice_in_dim(query_float, anchor, TOK_DEV, 0)
        cotangent_block = lax.dynamic_slice_in_dim(cotangent_float, anchor, TOK_DEV, 0)
        reach_block = lax.dynamic_slice_in_dim(reach_back, anchor, TOK_DEV, 0)
        key_block = lax.dynamic_slice_in_dim(padded_keys, anchor, window, 1)
        value_block = lax.dynamic_slice_in_dim(padded_values, anchor, window, 1)
        query_places = anchor + jnp.arange(TOK_DEV, dtype=jnp.int32)
        key_places = anchor - SPAN + jnp.arange(window, dtype=jnp.int32)
        distance = query_places[:, None] - key_places[None, :]
        allowed = (key_places[None, :] >= 0) & (distance >= 0) & (distance < reach_block[:, None])
        scores = jnp.einsum('tgjd,gkd->gjtk', query_block, key_block) * score_scale
        masked = jnp.where(allowed, scores, -jnp.inf)
        row_max = lax.optimization_barrier(jnp.max(masked, axis=-1, keepdims=True))
        log_norm = row_max + jnp.log(lax.optimization_barrier(jnp.sum(jnp.exp(masked - row_max), axis=-1, keepdims=True)))
        soft_probs = jnp.where(allowed, jnp.exp(scores - log_norm), 0.0)
        soft_weights = soft_probs.astype(jnp.bfloat16)
        dot_part = jnp.einsum('tgjd,gkd->gjtk', cotangent_block, value_block)
        dot_total = lax.optimization_barrier(jnp.sum(soft_probs * dot_part, axis=-1, keepdims=True))
        score_gradient = (soft_probs * (dot_part - dot_total) * score_scale).astype(jnp.bfloat16)
        key_gradient = jnp.einsum('gjtk,tgjd->gkd', score_gradient.astype(jnp.float32), query_block)
        value_gradient = jnp.einsum('gjtk,tgjd->gkd', soft_weights.astype(jnp.float32), cotangent_block)
        return jnp.stack([key_gradient, value_gradient], axis=1)

    def accumulate(running, number):
        anchor = (number * TOK_DEV).astype(jnp.int32)
        current = lax.dynamic_slice_in_dim(running, anchor, window, 2)
        running = lax.dynamic_update_slice_in_dim(running, current + window_grads(anchor), anchor, 2)
        return (running, None)
    running = jnp.zeros((KVH, 2, SPAN + TOKENS, HD), jnp.float32)
    running, unused = lax.scan(accumulate, running, jnp.arange(TOKENS // TOK_DEV, dtype=jnp.int32))
    gradients = running[:, :, SPAN:, :]
    key_total = jnp.zeros((CW, HD), jnp.float32).at[code_ids[:, 0, :].reshape(-1)].add(gradients[:, 0].reshape(-1, HD))
    value_total = jnp.zeros((CW, HD), jnp.float32).at[code_ids[:, 1, :].reshape(-1)].add(gradients[:, 1].reshape(-1, HD))
    return jnp.stack([key_total, value_total])
```

```python
import math

import jax
import jax.numpy as jnp
from jax import lax
from jax.experimental import pallas as pl
from jax.experimental.pallas import tpu as pltpu
from jax.sharding import PartitionSpec as P

MESH = pl.DeviceIdType.MESH
SPAN = 768
XN, YLO, YHI, ZN = 4, 4, 2, 8
YN = YLO * YHI
F32, BF16 = jnp.float32, jnp.bfloat16


def nn(a, b):
    return lax.dot_general(a, b, (((1,), (0,)), ((), ())), preferred_element_type=F32)


def nt(a, b):
    return lax.dot_general(a, b, (((1,), (1,)), ((), ())), preferred_element_type=F32)


def split_halves(a, b):
    low = lax.broadcasted_iota(jnp.int32, a.shape, 1) < 4
    return (
        jnp.where(low, a, pltpu.roll(b, 4, 1)),
        jnp.where(low, pltpu.roll(a, 4, 1), b),
    )


def kernel(
    q_ref, g_ref, cb_ref, ids_ref, reach_ref, out_ref,
    cbt, onehot, rows, grads, low_ref, ids_all, keep, csend, crecv, xsend, xrecv, xown,
    ysend, yrecv, yred, zsend, zrecv,
    id_s, id_r, c_s, c_r, x_s, x_r, y_s, y_r, z_s, z_r,
):
    tok = reach_ref.shape[1]
    words, width = cb_ref.shape[1], cb_ref.shape[2]
    n_rows = q_ref.shape[0]
    group = n_rows // tok
    blocks = SPAN // tok + 1
    scale = 1.0 / math.sqrt(width)
    seq, head = lax.axis_index("seq"), lax.axis_index("head")
    n_seq = lax.axis_size("seq")
    z = seq % ZN
    x = (seq // ZN) % XN
    y_lo = seq // (ZN * XN)
    y_hi, core = head // 2, head % 2
    y = y_hi * YLO + y_lo

    def device(x_at, y_at, z_at, core_at):
        return (((y_at % YLO) * XN + x_at) * ZN + z_at, (y_at // YLO) * 2 + core_at)

    buddy = device(x, y, z, 1 - core)
    x_peers = [device((x + i) % XN, y, z, core) for i in range(1, XN)]
    y_peers = [device(x, (y + i) % YN, z, core) for i in range(1, YN)]
    z_peers = [device(x, y, (z + i) % ZN, core) for i in range(1, ZN)]
    ahead = [((seq + i) % n_seq, head) for i in range(1, blocks)]
    behind = [((seq + n_seq - i) % n_seq, head) for i in range(1, blocks)]

    barrier = pltpu.get_barrier_semaphore()
    greeted = [buddy] + x_peers + y_peers + z_peers + behind
    for peer in greeted:
        pl.semaphore_signal(barrier, inc=1, device_id=peer, device_id_type=MESH)

    seg = words // 16
    for s in range(16):
        base = (s % YLO) * (seg * XN) + (s // YLO) * seg
        for table in range(2):
            cbt[table, :, s * seg : (s + 1) * seg] = cb_ref[table, base : base + seg, :].T

    tiles = 8
    tile_tok = tok // tiles
    lanes = tile_tok * group
    place = seq * tok + lax.broadcasted_iota(jnp.int32, (1, tok), 1)
    reach = jnp.minimum(reach_ref[...], place + 1)
    at_tile = lax.broadcasted_iota(jnp.int32, (tiles, tok), 1) // tile_tok == lax.broadcasted_iota(
        jnp.int32, (tiles, tok), 0
    )
    spread = (
        lax.broadcasted_iota(jnp.int32, (tok, lanes), 0) % tile_tok
        == lax.broadcasted_iota(jnp.int32, (tok, lanes), 1) // group
    ).astype(F32).astype(BF16)

    def expand(part):
        return nn(jnp.where(at_tile, part.astype(F32), 0.0).astype(BF16), spread)

    tau = lax.broadcasted_iota(jnp.int32, (1, lanes), 1) // group
    reach_wide = (expand(reach // 256) * 256.0 + expand(reach % 256)).astype(jnp.int32)
    low_ref[...] = SPAN + tau - reach_wide

    ids_all[blocks - 1] = ids_ref[...]
    grads[...] = jnp.zeros_like(grads)

    pl.semaphore_wait(barrier, len(greeted))

    id_copies = []
    for i in range(blocks - 1):
        copy = pltpu.make_async_remote_copy(
            src_ref=ids_ref,
            dst_ref=ids_all.at[blocks - 2 - i],
            send_sem=id_s.at[i],
            recv_sem=id_r.at[i],
            device_id=ahead[i],
            device_id_type=MESH,
        )
        copy.start()
        id_copies.append(copy)

    def decode(block):
        cols = slice(block * tok, (block + 1) * tok)
        for table in range(2):
            ids = ids_all[block, table : table + 1, :]
            for s in range(16):
                base = (s % YLO) * (seg * XN) + (s // YLO) * seg
                word = base + lax.broadcasted_iota(jnp.int32, (seg, tok), 0)
                onehot[table, s * seg : (s + 1) * seg, cols] = (
                    (word == ids).astype(F32).astype(BF16)
                )
            rows[table, cols, :] = nn(cbt[table], onehot[table, :, cols]).T.astype(BF16)

    decode(blocks - 1)
    for i in range(blocks - 1):
        id_copies[i].wait()
    for block in range(blocks - 1):
        decode(block)

    win = SPAN + tile_tok

    def tile_step(a, carry):
        at = pl.ds(pl.multiple_of(a * lanes, lanes), lanes)
        keys = pl.ds(pl.multiple_of(a * tile_tok, tile_tok), win)
        q, g = q_ref[at, :], g_ref[at, :]
        low = low_ref[pl.ds(a, 1), :]
        index = lax.broadcasted_iota(jnp.int32, (win, lanes), 0)
        allowed = (index > low) & (index <= SPAN + tau)
        s = jnp.where(allowed, nt(rows[0, keys, :], q), -1e30)
        top = jnp.max(s, axis=0, keepdims=True)
        c = scale * math.log2(math.e)
        p = jnp.exp2((s - top) * c)
        inv = 1.0 / jnp.sum(p, axis=0, keepdims=True)
        d = nt(rows[1, keys, :], g)
        total = jnp.sum(p * d, axis=0, keepdims=True) * inv
        w = p * inv
        e = (w * (d - total) * scale).astype(BF16)
        grads[0, keys, :] += nn(e, q)
        grads[1, keys, :] += nn(w.astype(BF16), g)
        return carry

    lax.fori_loop(0, tiles, tile_step, 0)

    half = words // XN // 2
    upper = [grads[table].astype(BF16) for table in range(2)]
    order = (2, 1, 3, 0)
    c_copies = {}
    for i in order:
        x_to = (x + i) % XN
        for table in range(2):
            at = pl.ds(pl.multiple_of(x_to * (words // XN), words // XN), words // XN)
            part = nn(onehot[table, at, :], upper[table]).reshape(half // 8, 16, width)
            first, second = split_halves(part[:, :8, :], part[:, 8:, :])
            first, second = first.reshape(half, width), second.reshape(half, width)
            keep[i, table * half : (table + 1) * half, :] = jnp.where(core == 0, first, second)
            csend[i, table * half : (table + 1) * half, :] = jnp.where(
                core == 0, second, first
            ).astype(BF16)
        copy = pltpu.make_async_remote_copy(
            src_ref=csend.at[i],
            dst_ref=crecv.at[i],
            send_sem=c_s.at[i],
            recv_sem=c_r.at[i],
            device_id=buddy,
            device_id_type=MESH,
        )
        copy.start()
        c_copies[i] = copy

    x_copies = []
    for i in order:
        c_copies[i].wait()
        chip = keep[i] + crecv[i].astype(F32)
        if i == 0:
            xown[...] = chip
            continue
        xsend[i - 1] = chip.astype(BF16)
        copy = pltpu.make_async_remote_copy(
            src_ref=xsend.at[i - 1],
            dst_ref=xrecv.at[i - 1],
            send_sem=x_s.at[i - 1],
            recv_sem=x_r.at[i - 1],
            device_id=x_peers[i - 1],
            device_id_type=MESH,
        )
        copy.start()
        x_copies.append(copy)
    for copy in x_copies:
        copy.wait()

    line = xown[...]
    for i in range(XN - 1):
        line = line + xrecv[i].astype(F32)
    line = line.reshape(2, half // 8, 8, width)
    for at_hi, part in enumerate(split_halves(line[0], line[1])):
        yred[at_hi * YLO : (at_hi + 1) * YLO] = part.reshape(YLO, ZN * 8, width)
    ysend[...] = yred[...].astype(BF16)
    y_copies = []
    for i in range(1, YN):
        copy = pltpu.make_async_remote_copy(
            src_ref=ysend.at[(y + i) % YN],
            dst_ref=yrecv.at[i - 1],
            send_sem=y_s.at[i - 1],
            recv_sem=y_r.at[i - 1],
            device_id=y_peers[i - 1],
            device_id_type=MESH,
        )
        copy.start()
        y_copies.append(copy)
    for copy in y_copies:
        copy.wait()
    plane = yred[y]
    for i in range(YN - 1):
        plane = plane + yrecv[i].astype(F32)
    zsend[...] = plane.reshape(ZN, 8, width)
    z_copies = []
    for i in range(1, ZN):
        copy = pltpu.make_async_remote_copy(
            src_ref=zsend.at[(z + i) % ZN],
            dst_ref=zrecv.at[i - 1],
            send_sem=z_s.at[i - 1],
            recv_sem=z_r.at[i - 1],
            device_id=z_peers[i - 1],
            device_id_type=MESH,
        )
        copy.start()
        z_copies.append(copy)
    for copy in z_copies:
        copy.wait()
    done = zsend[z]
    for i in range(ZN - 1):
        done = done + zrecv[i]
    out_ref[...] = done


def on_device(queries, out_gradient, codebook, code_ids, reach_back):
    tok, heads, width = queries.shape
    words = codebook.shape[1]
    blocks = SPAN // tok + 1
    half = words // XN // 2
    dma = pltpu.SemaphoreType.DMA
    out = pl.pallas_call(
        kernel,
        out_shape=jax.ShapeDtypeStruct((8, width), F32),
        in_specs=[pl.BlockSpec(memory_space=pltpu.VMEM)] * 5,
        out_specs=pl.BlockSpec(memory_space=pltpu.VMEM),
        scratch_shapes=[
            pltpu.VMEM((2, width, words), BF16),
            pltpu.VMEM((2, words, blocks * tok), BF16),
            pltpu.VMEM((2, blocks * tok, width), BF16),
            pltpu.VMEM((2, blocks * tok, width), F32),
            pltpu.VMEM((8, tok), jnp.int32),
            pltpu.VMEM((blocks, 2, tok), jnp.int32),
            pltpu.VMEM((XN, 2 * half, width), F32),
            pltpu.VMEM((XN, 2 * half, width), BF16),
            pltpu.VMEM((XN, 2 * half, width), BF16),
            pltpu.VMEM((XN - 1, 2 * half, width), BF16),
            pltpu.VMEM((XN - 1, 2 * half, width), BF16),
            pltpu.VMEM((2 * half, width), F32),
            pltpu.VMEM((YN, ZN * 8, width), BF16),
            pltpu.VMEM((YN - 1, ZN * 8, width), BF16),
            pltpu.VMEM((YN, ZN * 8, width), F32),
            pltpu.VMEM((ZN, 8, width), F32),
            pltpu.VMEM((ZN - 1, 8, width), F32),
            dma((blocks - 1,)), dma((blocks - 1,)),
            dma((XN,)), dma((XN,)),
            dma((XN - 1,)), dma((XN - 1,)),
            dma((YN - 1,)), dma((YN - 1,)),
            dma((ZN - 1,)), dma((ZN - 1,)),
        ],
        compiler_params=pltpu.CompilerParams(
            collective_id=0, has_side_effects=True, vmem_limit_bytes=48 * 2**20
        ),
    )(
        queries.reshape(tok * heads, width),
        out_gradient.reshape(tok * heads, width),
        codebook,
        code_ids.reshape(2, tok),
        reach_back.reshape(1, tok),
    )
    return out.reshape(2, 4, width)


def solution(mesh):
    in_specs = (
        P("seq", "head", None),
        P("seq", "head", None),
        P(),
        P("head", None, "seq"),
        P("seq"),
    )
    out_specs = P(None, ("seq", "head"), None)
    return jax.shard_map(
        on_device, mesh=mesh, in_specs=in_specs, out_specs=out_specs, check_vma=False
    )
```

```python
import math

import jax
import jax.numpy as jnp
from jax import lax
from jax.experimental import pallas as pl
from jax.experimental.pallas import tpu as pltpu
from jax.sharding import PartitionSpec as P

MESH = pl.DeviceIdType.MESH
SPAN = 768
XN, YLO, YHI, ZN = 4, 4, 2, 8
YN = YLO * YHI
HIGH, LOW = 8, 256
TILES = 8
F32, BF16 = jnp.float32, jnp.bfloat16


def nn(a, b):
    return lax.dot_general(a, b, (((1,), (0,)), ((), ())), preferred_element_type=F32)


def nt(a, b):
    return lax.dot_general(a, b, (((1,), (1,)), ((), ())), preferred_element_type=F32)


def split_halves(a, b):
    low = lax.broadcasted_iota(jnp.int32, a.shape, 1) < 4
    return (
        jnp.where(low, a, pltpu.roll(b, 4, 1)),
        jnp.where(low, pltpu.roll(a, 4, 1), b),
    )


def kernel(
    q_hbm, g_hbm, cb_hbm, ids_hbm, reach_hbm, out_ref,
    q_ref, g_ref, cb_ref, reach_ref, ids_all,
    cbt, onehot, high, rows, grads, low_ref, part_ref,
    keep, csend, crecv, xsend, xrecv, ysend, yrecv, yred, zsend, zrecv,
    in_s, id_s, id_r, c_s, c_r, x_s, x_r, y_s, y_r, z_s, z_r,
):
    tok = reach_ref.shape[1]
    words, width = cb_ref.shape[1], cb_ref.shape[2]
    n_rows = q_ref.shape[0]
    group = n_rows // tok
    blocks = SPAN // tok + 1
    scale = 1.0 / math.sqrt(width)
    seq, head = lax.axis_index("seq"), lax.axis_index("head")
    n_seq = lax.axis_size("seq")
    z = seq % ZN
    x = (seq // ZN) % XN
    x_hi, x_lo = x // 2, x % 2
    y_lo = seq // (ZN * XN)
    y_hi, core = head // 2, head % 2
    y = y_hi * YLO + y_lo

    def device(x_at, y_at, z_at, core_at):
        return (((y_at % YLO) * XN + x_at) * ZN + z_at, (y_at // YLO) * 2 + core_at)

    def x_other(j):
        hi = 1 - x_hi if j // 2 else x_hi
        lo = 1 - x_lo if j % 2 else x_lo
        return hi * 2 + lo

    buddy = device(x, y, z, 1 - core)
    x_peers = [device(x_other(j), y, z, core) for j in range(1, XN)]
    y_peers = [device(x, (y + i) % YN, z, core) for i in range(1, YN)]
    z_peers = [device(x, y, (z + i) % ZN, core) for i in range(1, ZN)]
    ahead = [((seq + i) % n_seq, head) for i in range(1, blocks)]
    behind = [((seq + n_seq - i) % n_seq, head) for i in range(1, blocks)]

    barrier = pltpu.get_barrier_semaphore()
    greeted = [buddy] + x_peers + y_peers + z_peers + behind
    for peer in greeted:
        pl.semaphore_signal(barrier, inc=1, device_id=peer, device_id_type=MESH)

    loads = [
        pltpu.make_async_copy(src, dst, in_s.at[i])
        for i, (src, dst) in enumerate(
            (
                (ids_hbm, ids_all.at[blocks - 1]),
                (reach_hbm, reach_ref),
                (cb_hbm, cb_ref),
                (q_hbm, q_ref),
                (g_hbm, g_ref),
            )
        )
    ]
    for load in loads:
        load.start()
    grads[...] = jnp.zeros_like(grads)

    tile_tok = tok // TILES
    lanes = tile_tok * group
    tau = lax.broadcasted_iota(jnp.int32, (1, lanes), 1) // group
    at_tile = lax.broadcasted_iota(jnp.int32, (TILES, tok), 1) // tile_tok == lax.broadcasted_iota(
        jnp.int32, (TILES, tok), 0
    )
    spread = (
        lax.broadcasted_iota(jnp.int32, (tok, lanes), 0) % tile_tok
        == lax.broadcasted_iota(jnp.int32, (tok, lanes), 1) // group
    ).astype(F32).astype(BF16)

    def expand(part):
        return nn(jnp.where(at_tile, part.astype(F32), 0.0).astype(BF16), spread)

    loads[0].wait()
    loads[1].wait()
    place = seq * tok + lax.broadcasted_iota(jnp.int32, (1, tok), 1)
    reach = jnp.minimum(reach_ref[...], place + 1)
    reach_wide = (expand(reach // 256) * 256.0 + expand(reach % 256)).astype(jnp.int32)
    low_ref[...] = SPAN + tau - reach_wide

    loads[2].wait()
    for table in range(2):
        for h in range(HIGH):
            cbt[table, h * width : (h + 1) * width, :] = cb_ref[
                table, h * LOW : (h + 1) * LOW, :
            ].T

    pl.semaphore_wait(barrier, len(greeted))

    id_copies = []
    for i in range(blocks - 1):
        copy = pltpu.make_async_remote_copy(
            src_ref=ids_all.at[blocks - 1],
            dst_ref=ids_all.at[blocks - 2 - i],
            send_sem=id_s.at[i],
            recv_sem=id_r.at[i],
            device_id=ahead[i],
            device_id_type=MESH,
        )
        copy.start()
        id_copies.append(copy)

    def decode(block):
        cols = slice(block * tok, (block + 1) * tok)
        ids = ids_all[block]
        hi = ids // LOW
        columns = jnp.concatenate(
            [hi.astype(F32), jnp.zeros((6, tok), F32)], axis=0
        ).T
        word = lax.broadcasted_iota(jnp.int32, (LOW, tok), 0)
        for table in range(2):
            onehot[table, :, cols] = (
                (word == ids[table : table + 1, :] % LOW).astype(F32).astype(BF16)
            )
            high[table, cols, :] = jnp.broadcast_to(
                columns[:, table : table + 1], (tok, width)
            ).astype(BF16)
            found = nn(cbt[table], onehot[table, :, cols])
            own = found[:width]
            for h in range(1, HIGH):
                own = jnp.where(
                    hi[table : table + 1, :] == h, found[h * width : (h + 1) * width], own
                )
            rows[table, cols, :] = own.T.astype(BF16)

    decode(blocks - 1)
    for load in loads[3:]:
        load.wait()
    for i in range(blocks - 1):
        id_copies[i].wait()
        decode(blocks - 2 - i)

    win = SPAN + tile_tok

    def tile_step(a, carry):
        at = pl.ds(pl.multiple_of(a * lanes, lanes), lanes)
        keys = pl.ds(pl.multiple_of(a * tile_tok, tile_tok), win)
        q, g = q_ref[at, :], g_ref[at, :]
        low = low_ref[pl.ds(a, 1), :]
        index = lax.broadcasted_iota(jnp.int32, (win, lanes), 0)
        s = jnp.where(index > low, nt(rows[0, keys, :], q), -1e30)
        last = jnp.where(index[:tile_tok] <= tau, s[SPAN:], -1e30)
        s = jnp.concatenate([s[:SPAN], last], axis=0)
        top = jnp.max(s, axis=0, keepdims=True)
        p = jnp.exp2((s - top) * (scale * math.log2(math.e)))
        inv = 1.0 / jnp.sum(p, axis=0, keepdims=True)
        d = nt(rows[1, keys, :], g)
        total = jnp.sum(p * d, axis=0, keepdims=True) * inv
        e = ((p * (inv * scale)) * (d - total)).astype(BF16)
        w = (p * inv).astype(BF16)
        grads[0, keys, :] += nn(e, q)
        grads[1, keys, :] += nn(w, g)
        return carry

    lax.fori_loop(0, TILES, tile_step, 0, unroll=2)

    half = words // XN // 2
    y_rows = half // YLO
    c_copies = {}
    for flip in (1, 0):
        at_hi = 1 - x_hi if flip else x_hi
        for table in range(2):
            part = grads[table].astype(BF16)
            wide = jnp.concatenate(
                [
                    jnp.where(
                        high[table] == (at_y * 2 + at_hi).astype(F32).astype(BF16),
                        part,
                        jnp.zeros_like(part),
                    )
                    for at_y in range(YLO)
                ],
                axis=1,
            )
            part_ref[table] = nn(onehot[table], wide)
        for j in (flip * 2 + 1, flip * 2):
            at_lo = 1 - x_lo if j % 2 else x_lo
            span = pl.ds(pl.multiple_of(at_lo * (LOW // 2), LOW // 2), LOW // 2)
            for table in range(2):
                for at_y in range(YLO):
                    part = part_ref[table, span, at_y * width : (at_y + 1) * width]
                    part = part.reshape(LOW // 32, 16, width)
                    first, second = split_halves(part[:, :8, :], part[:, 8:, :])
                    first, second = first.reshape(y_rows, width), second.reshape(y_rows, width)
                    to = slice(table * half + at_y * y_rows, table * half + (at_y + 1) * y_rows)
                    keep[j, to, :] = jnp.where(core == 0, first, second)
                    csend[j, to, :] = jnp.where(core == 0, second, first).astype(BF16)
            copy = pltpu.make_async_remote_copy(
                src_ref=csend.at[j],
                dst_ref=crecv.at[j],
                send_sem=c_s.at[j],
                recv_sem=c_r.at[j],
                device_id=buddy,
                device_id_type=MESH,
            )
            copy.start()
            c_copies[j] = copy

    x_copies = []
    for j in (3, 2, 1):
        c_copies[j].wait()
        xsend[j - 1] = (keep[j] + crecv[j].astype(F32)).astype(BF16)
        copy = pltpu.make_async_remote_copy(
            src_ref=xsend.at[j - 1],
            dst_ref=xrecv.at[j - 1],
            send_sem=x_s.at[j - 1],
            recv_sem=x_r.at[j - 1],
            device_id=x_peers[j - 1],
            device_id_type=MESH,
        )
        copy.start()
        x_copies.append(copy)
    c_copies[0].wait()
    for copy in x_copies:
        copy.wait()

    line = keep[0] + crecv[0].astype(F32)
    for i in range(XN - 1):
        line = line + xrecv[i].astype(F32)
    line = line.reshape(2, half // 8, 8, width)
    for at_hi, part in enumerate(split_halves(line[0], line[1])):
        yred[at_hi * YLO : (at_hi + 1) * YLO] = part.reshape(YLO, ZN * 8, width)
    ysend[...] = yred[...].astype(BF16)
    y_copies = []
    for i in range(1, YN):
        copy = pltpu.make_async_remote_copy(
            src_ref=ysend.at[(y + i) % YN],
            dst_ref=yrecv.at[i - 1],
            send_sem=y_s.at[i - 1],
            recv_sem=y_r.at[i - 1],
            device_id=y_peers[i - 1],
            device_id_type=MESH,
        )
        copy.start()
        y_copies.append(copy)
    for copy in y_copies:
        copy.wait()
    plane = yred[y]
    for i in range(YN - 1):
        plane = plane + yrecv[i].astype(F32)
    zsend[...] = plane.reshape(ZN, 8, width)
    z_copies = []
    for i in range(1, ZN):
        copy = pltpu.make_async_remote_copy(
            src_ref=zsend.at[(z + i) % ZN],
            dst_ref=zrecv.at[i - 1],
            send_sem=z_s.at[i - 1],
            recv_sem=z_r.at[i - 1],
            device_id=z_peers[i - 1],
            device_id_type=MESH,
        )
        copy.start()
        z_copies.append(copy)
    for copy in z_copies:
        copy.wait()
    done = zsend[z]
    for i in range(ZN - 1):
        done = done + zrecv[i]
    out_ref[...] = done


def on_device(queries, out_gradient, codebook, code_ids, reach_back):
    tok, heads, width = queries.shape
    words = codebook.shape[1]
    blocks = SPAN // tok + 1
    half = words // XN // 2
    dma = pltpu.SemaphoreType.DMA
    out = pl.pallas_call(
        kernel,
        out_shape=jax.ShapeDtypeStruct((8, width), F32),
        in_specs=[pl.BlockSpec(memory_space=pl.ANY)] * 5,
        out_specs=pl.BlockSpec(memory_space=pltpu.VMEM),
        scratch_shapes=[
            pltpu.VMEM((tok * heads, width), BF16),
            pltpu.VMEM((tok * heads, width), BF16),
            pltpu.VMEM((2, words, width), BF16),
            pltpu.VMEM((1, tok), jnp.int32),
            pltpu.VMEM((blocks, 2, tok), jnp.int32),
            pltpu.VMEM((2, HIGH * width, LOW), BF16),
            pltpu.VMEM((2, LOW, blocks * tok), BF16),
            pltpu.VMEM((2, blocks * tok, width), BF16),
            pltpu.VMEM((2, blocks * tok, width), BF16),
            pltpu.VMEM((2, blocks * tok, width), F32),
            pltpu.VMEM((TILES, tok), jnp.int32),
            pltpu.VMEM((2, LOW, YLO * width), F32),
            pltpu.VMEM((XN, 2 * half, width), F32),
            pltpu.VMEM((XN, 2 * half, width), BF16),
            pltpu.VMEM((XN, 2 * half, width), BF16),
            pltpu.VMEM((XN - 1, 2 * half, width), BF16),
            pltpu.VMEM((XN - 1, 2 * half, width), BF16),
            pltpu.VMEM((YN, ZN * 8, width), BF16),
            pltpu.VMEM((YN - 1, ZN * 8, width), BF16),
            pltpu.VMEM((YN, ZN * 8, width), F32),
            pltpu.VMEM((ZN, 8, width), F32),
            pltpu.VMEM((ZN - 1, 8, width), F32),
            dma((5,)),
            dma((blocks - 1,)), dma((blocks - 1,)),
            dma((XN,)), dma((XN,)),
            dma((XN - 1,)), dma((XN - 1,)),
            dma((YN - 1,)), dma((YN - 1,)),
            dma((ZN - 1,)), dma((ZN - 1,)),
        ],
        compiler_params=pltpu.CompilerParams(
            collective_id=0, has_side_effects=True, vmem_limit_bytes=56 * 2**20
        ),
    )(
        queries.reshape(tok * heads, width),
        out_gradient.reshape(tok * heads, width),
        codebook,
        code_ids.reshape(2, tok),
        reach_back.reshape(1, tok),
    )
    return out.reshape(2, 4, width)


def solution(mesh):
    in_specs = (
        P("seq", "head", None),
        P("seq", "head", None),
        P(),
        P("head", None, "seq"),
        P("seq"),
    )
    out_specs = P(None, ("seq", "head"), None)
    return jax.shard_map(
        on_device, mesh=mesh, in_specs=in_specs, out_specs=out_specs, check_vma=False
    )
```

```python
import math

import jax
import jax.numpy as jnp
from jax import lax
from jax.experimental import pallas as pl
from jax.experimental.pallas import tpu as pltpu
from jax.sharding import PartitionSpec as P

MESH = pl.DeviceIdType.MESH
SPAN = 768
XN, YLO, YHI, ZN = 4, 4, 2, 8
YN = YLO * YHI
HIGH, LOW = 8, 256
TILES = 8
F32, BF16 = jnp.float32, jnp.bfloat16


def nn(a, b):
    return lax.dot_general(a, b, (((1,), (0,)), ((), ())), preferred_element_type=F32)


def nt(a, b):
    return lax.dot_general(a, b, (((1,), (1,)), ((), ())), preferred_element_type=F32)


def split_halves(a, b):
    low = lax.broadcasted_iota(jnp.int32, a.shape, 1) < 4
    return (
        jnp.where(low, a, pltpu.roll(b, 4, 1)),
        jnp.where(low, pltpu.roll(a, 4, 1), b),
    )


def kernel(
    q_hbm, g_hbm, cb_hbm, ids_hbm, reach_hbm, out_ref,
    q_ref, g_ref, cb_ref, reach_ref, ids_all,
    cbt, onehot, high, rows, grads, low_ref, part_ref, s_ref, d_ref, e_ref, w_ref,
    keep, csend, crecv, xsend, xrecv, ysend, yrecv, yred, zsend, zrecv,
    in_s, id_s, id_r, c_s, c_r, x_s, x_r, y_s, y_r, z_s, z_r,
):
    tok = reach_ref.shape[1]
    words, width = cb_ref.shape[1], cb_ref.shape[2]
    n_rows = q_ref.shape[0]
    group = n_rows // tok
    blocks = SPAN // tok + 1
    scale = 1.0 / math.sqrt(width)
    seq, head = lax.axis_index("seq"), lax.axis_index("head")
    n_seq = lax.axis_size("seq")
    z = seq % ZN
    x = (seq // ZN) % XN
    x_hi, x_lo = x // 2, x % 2
    y_lo = seq // (ZN * XN)
    y_hi, core = head // 2, head % 2
    y = y_hi * YLO + y_lo

    def device(x_at, y_at, z_at, core_at):
        return (((y_at % YLO) * XN + x_at) * ZN + z_at, (y_at // YLO) * 2 + core_at)

    def x_other(j):
        hi = 1 - x_hi if j // 2 else x_hi
        lo = 1 - x_lo if j % 2 else x_lo
        return hi * 2 + lo

    buddy = device(x, y, z, 1 - core)
    x_peers = [device(x_other(j), y, z, core) for j in range(1, XN)]
    y_peers = [device(x, (y + i) % YN, z, core) for i in range(1, YN)]
    z_peers = [device(x, y, (z + i) % ZN, core) for i in range(1, ZN)]
    ahead = [((seq + i) % n_seq, head) for i in range(1, blocks)]
    behind = [((seq + n_seq - i) % n_seq, head) for i in range(1, blocks)]

    barrier = pltpu.get_barrier_semaphore()
    greeted = behind + z_peers + y_peers + x_peers + [buddy]
    for peer in greeted:
        pl.semaphore_signal(barrier, inc=1, device_id=peer, device_id_type=MESH)

    loads = [
        pltpu.make_async_copy(src, dst, in_s.at[i])
        for i, (src, dst) in enumerate(
            (
                (ids_hbm, ids_all.at[blocks - 1]),
                (reach_hbm, reach_ref),
                (cb_hbm, cb_ref),
                (q_hbm, q_ref),
                (g_hbm, g_ref),
            )
        )
    ]
    for load in loads:
        load.start()
    grads[...] = jnp.zeros_like(grads)

    tile_tok = tok // TILES
    lanes = tile_tok * group
    tau = lax.broadcasted_iota(jnp.int32, (1, lanes), 1) // group
    at_tile = lax.broadcasted_iota(jnp.int32, (TILES, tok), 1) // tile_tok == lax.broadcasted_iota(
        jnp.int32, (TILES, tok), 0
    )
    spread = (
        lax.broadcasted_iota(jnp.int32, (tok, lanes), 0) % tile_tok
        == lax.broadcasted_iota(jnp.int32, (tok, lanes), 1) // group
    ).astype(F32).astype(BF16)

    def expand(part):
        return nn(jnp.where(at_tile, part.astype(F32), 0.0).astype(BF16), spread)

    loads[0].wait()
    loads[1].wait()
    place = seq * tok + lax.broadcasted_iota(jnp.int32, (1, tok), 1)
    reach = jnp.minimum(reach_ref[...], place + 1)
    reach_wide = (expand(reach // 256) * 256.0 + expand(reach % 256)).astype(jnp.int32)
    low_ref[...] = SPAN + tau - reach_wide

    loads[2].wait()
    for table in range(2):
        for h in range(HIGH):
            cbt[table, h * width : (h + 1) * width, :] = cb_ref[
                table, h * LOW : (h + 1) * LOW, :
            ].T

    pl.semaphore_wait(barrier, len(greeted))

    id_copies = []
    for i in range(blocks - 1):
        copy = pltpu.make_async_remote_copy(
            src_ref=ids_all.at[blocks - 1],
            dst_ref=ids_all.at[blocks - 2 - i],
            send_sem=id_s.at[i],
            recv_sem=id_r.at[i],
            device_id=ahead[i],
            device_id_type=MESH,
        )
        copy.start()
        id_copies.append(copy)

    def decode(block):
        cols = slice(block * tok, (block + 1) * tok)
        ids = ids_all[block]
        hi = ids // LOW
        columns = jnp.concatenate(
            [hi.astype(F32), jnp.zeros((6, tok), F32)], axis=0
        ).T
        word = lax.broadcasted_iota(jnp.int32, (LOW, tok), 0)
        for table in range(2):
            onehot[table, :, cols] = (
                (word == ids[table : table + 1, :] % LOW).astype(F32).astype(BF16)
            )
            high[table, cols, :] = jnp.broadcast_to(
                columns[:, table : table + 1], (tok, width)
            ).astype(BF16)
            found = nn(cbt[table], onehot[table, :, cols])
            own = found[:width]
            for h in range(1, HIGH):
                own = jnp.where(
                    hi[table : table + 1, :] == h, found[h * width : (h + 1) * width], own
                )
            rows[table, cols, :] = own.T.astype(BF16)

    decode(blocks - 1)
    for load in loads[3:]:
        load.wait()
    for i in range(blocks - 1):
        id_copies[i].wait()
        decode(blocks - 2 - i)

    win = SPAN + tile_tok
    step = tile_tok
    steps = win // step
    ramp = lax.broadcasted_iota(jnp.int32, (step, lanes), 0)
    inverse = {}

    def queries_of(a):
        return slice(a * lanes, (a + 1) * lanes)

    def keys_of(a):
        return slice(a * tile_tok, a * tile_tok + win)

    def part_of(j):
        return slice(j * step, (j + 1) * step)

    def softmax(a):
        low = low_ref[a : a + 1, :] - ramp
        top = None
        for j in range(steps):
            s = jnp.where(low < j * step, s_ref[a, part_of(j), :], -1e30)
            if j == steps - 1:
                s = jnp.where(ramp <= tau, s, -1e30)
            s_ref[a, part_of(j), :] = s
            top = s if j == 0 else jnp.maximum(top, s)
        top = jnp.max(top, axis=0, keepdims=True)
        norm = jnp.zeros((step, lanes), F32)
        for j in range(steps):
            p = jnp.exp2((s_ref[a, part_of(j), :] - top) * (scale * math.log2(math.e)))
            s_ref[a, part_of(j), :] = p
            norm = norm + p
        inverse[a] = 1.0 / jnp.sum(norm, axis=0, keepdims=True)
        for j in range(steps):
            w_ref[a % 2, part_of(j), :] = (s_ref[a, part_of(j), :] * inverse[a]).astype(BF16)

    def score_gradient(a):
        total = jnp.zeros((step, lanes), F32)
        for j in range(steps):
            total = total + s_ref[a, part_of(j), :] * d_ref[a % 2, part_of(j), :]
        total = jnp.sum(total, axis=0, keepdims=True) * inverse[a]
        factor = inverse[a] * scale
        for j in range(steps):
            p, d = s_ref[a, part_of(j), :], d_ref[a % 2, part_of(j), :]
            e_ref[a % 2, part_of(j), :] = ((p * factor) * (d - total)).astype(BF16)

    def add_values(a):
        grads[1, keys_of(a), :] += nn(w_ref[a % 2], g_ref[queries_of(a), :])

    def add_keys(a):
        grads[0, keys_of(a), :] += nn(e_ref[a % 2], q_ref[queries_of(a), :])

    half = words // XN // 2
    y_rows = half // YLO
    c_copies, x_copies = {}, {}

    def scatter(table, flip):
        at_hi = 1 - x_hi if flip else x_hi
        part = grads[table].astype(BF16)
        wide = jnp.concatenate(
            [
                jnp.where(
                    high[table] == (at_y * 2 + at_hi).astype(F32).astype(BF16),
                    part,
                    jnp.zeros_like(part),
                )
                for at_y in range(YLO)
            ],
            axis=1,
        )
        part_ref[table] = nn(onehot[table], wide)

    def to_buddy(table, flip):
        for j in (flip * 2 + 1, flip * 2):
            at_lo = 1 - x_lo if j % 2 else x_lo
            span = pl.ds(pl.multiple_of(at_lo * (LOW // 2), LOW // 2), LOW // 2)
            for at_y in range(YLO):
                part = part_ref[table, span, at_y * width : (at_y + 1) * width]
                part = part.reshape(LOW // 32, 16, width)
                first, second = split_halves(part[:, :8, :], part[:, 8:, :])
                first, second = first.reshape(y_rows, width), second.reshape(y_rows, width)
                to = slice(at_y * y_rows, (at_y + 1) * y_rows)
                keep[table, j, to, :] = jnp.where(core == 0, first, second)
                csend[table, j, to, :] = jnp.where(core == 0, second, first).astype(BF16)
            copy = pltpu.make_async_remote_copy(
                src_ref=csend.at[table, j],
                dst_ref=crecv.at[table, j],
                send_sem=c_s.at[table, j],
                recv_sem=c_r.at[table, j],
                device_id=buddy,
                device_id_type=MESH,
            )
            copy.start()
            c_copies[table, j] = copy

    def to_x(table, j):
        c_copies[table, j].wait()
        xsend[table, j - 1] = (keep[table, j] + crecv[table, j].astype(F32)).astype(BF16)
        copy = pltpu.make_async_remote_copy(
            src_ref=xsend.at[table, j - 1],
            dst_ref=xrecv.at[table, j - 1],
            send_sem=x_s.at[table, j - 1],
            recv_sem=x_r.at[table, j - 1],
            device_id=x_peers[j - 1],
            device_id_type=MESH,
        )
        copy.start()
        x_copies[table, j] = copy

    def chip_line(table):
        c_copies[table, 0].wait()
        total = keep[table, 0] + crecv[table, 0].astype(F32)
        for j in (3, 2, 1):
            x_copies[table, j].wait()
            total = total + xrecv[table, j - 1].astype(F32)
        return total.reshape(half // 8, 8, width)

    for a in range(TILES):
        s_ref[a] = nt(rows[0, keys_of(a), :], q_ref[queries_of(a), :])
        if a > 0:
            add_values(a - 1)
        softmax(a)
    add_values(TILES - 1)
    for flip in (1, 0):
        scatter(1, flip)
        to_buddy(1, flip)
    for a in range(TILES):
        d_ref[a % 2] = nt(rows[1, keys_of(a), :], g_ref[queries_of(a), :])
        if a > 0:
            add_keys(a - 1)
        if a == 3:
            for j in (3, 2, 1):
                to_x(1, j)
        score_gradient(a)
    add_keys(TILES - 1)
    scatter(0, 1)
    to_buddy(0, 1)
    scatter(0, 0)
    to_x(0, 3)
    to_x(0, 2)
    to_buddy(0, 0)
    to_x(0, 1)
    value_line = chip_line(1)
    key_line = chip_line(0)
    for at_hi, part in enumerate(split_halves(key_line, value_line)):
        yred[at_hi * YLO : (at_hi + 1) * YLO] = part.reshape(YLO, ZN * 8, width)
    ysend[...] = yred[...].astype(BF16)
    y_copies = []
    for i in (4, 3, 5, 2, 6, 1, 7):
        copy = pltpu.make_async_remote_copy(
            src_ref=ysend.at[(y + i) % YN],
            dst_ref=yrecv.at[i - 1],
            send_sem=y_s.at[i - 1],
            recv_sem=y_r.at[i - 1],
            device_id=y_peers[i - 1],
            device_id_type=MESH,
        )
        copy.start()
        y_copies.append(copy)
    for copy in y_copies:
        copy.wait()
    plane = yred[y]
    for i in range(YN - 1):
        plane = plane + yrecv[i].astype(F32)
    zsend[...] = plane.reshape(ZN, 8, width)
    z_copies = []
    for i in (4, 3, 5, 2, 6, 1, 7):
        copy = pltpu.make_async_remote_copy(
            src_ref=zsend.at[(z + i) % ZN],
            dst_ref=zrecv.at[i - 1],
            send_sem=z_s.at[i - 1],
            recv_sem=z_r.at[i - 1],
            device_id=z_peers[i - 1],
            device_id_type=MESH,
        )
        copy.start()
        z_copies.append(copy)
    for copy in z_copies:
        copy.wait()
    done = zsend[z]
    for i in range(ZN - 1):
        done = done + zrecv[i]
    out_ref[...] = done


def on_device(queries, out_gradient, codebook, code_ids, reach_back):
    tok, heads, width = queries.shape
    words = codebook.shape[1]
    blocks = SPAN // tok + 1
    half = words // XN // 2
    dma = pltpu.SemaphoreType.DMA
    out = pl.pallas_call(
        kernel,
        out_shape=jax.ShapeDtypeStruct((8, width), F32),
        in_specs=[pl.BlockSpec(memory_space=pltpu.HBM)] * 5,
        out_specs=pl.BlockSpec(memory_space=pltpu.VMEM),
        scratch_shapes=[
            pltpu.VMEM((tok * heads, width), BF16),
            pltpu.VMEM((tok * heads, width), BF16),
            pltpu.VMEM((2, words, width), BF16),
            pltpu.VMEM((1, tok), jnp.int32),
            pltpu.VMEM((blocks, 2, tok), jnp.int32),
            pltpu.VMEM((2, HIGH * width, LOW), BF16),
            pltpu.VMEM((2, LOW, blocks * tok), BF16),
            pltpu.VMEM((2, blocks * tok, width), BF16),
            pltpu.VMEM((2, blocks * tok, width), BF16),
            pltpu.VMEM((2, blocks * tok, width), F32),
            pltpu.VMEM((TILES, tok), jnp.int32),
            pltpu.VMEM((2, LOW, YLO * width), F32),
            pltpu.VMEM((TILES, SPAN + tok // TILES, tok // TILES * heads), F32),
            pltpu.VMEM((2, SPAN + tok // TILES, tok // TILES * heads), F32),
            pltpu.VMEM((2, SPAN + tok // TILES, tok // TILES * heads), BF16),
            pltpu.VMEM((2, SPAN + tok // TILES, tok // TILES * heads), BF16),
            pltpu.VMEM((2, XN, half, width), F32),
            pltpu.VMEM((2, XN, half, width), BF16),
            pltpu.VMEM((2, XN, half, width), BF16),
            pltpu.VMEM((2, XN - 1, half, width), BF16),
            pltpu.VMEM((2, XN - 1, half, width), BF16),
            pltpu.VMEM((YN, ZN * 8, width), BF16),
            pltpu.VMEM((YN - 1, ZN * 8, width), BF16),
            pltpu.VMEM((YN, ZN * 8, width), F32),
            pltpu.VMEM((ZN, 8, width), F32),
            pltpu.VMEM((ZN - 1, 8, width), F32),
            dma((5,)),
            dma((blocks - 1,)), dma((blocks - 1,)),
            dma((2, XN)), dma((2, XN)),
            dma((2, XN - 1)), dma((2, XN - 1)),
            dma((YN - 1,)), dma((YN - 1,)),
            dma((ZN - 1,)), dma((ZN - 1,)),
        ],
        compiler_params=pltpu.CompilerParams(
            collective_id=0, has_side_effects=True, vmem_limit_bytes=56 * 2**20
        ),
    )(
        queries.reshape(tok * heads, width),
        out_gradient.reshape(tok * heads, width),
        codebook,
        code_ids.reshape(2, tok),
        reach_back.reshape(1, tok),
    )
    return out.reshape(2, 4, width)


def solution(mesh):
    in_specs = (
        P("seq", "head", None),
        P("seq", "head", None),
        P(),
        P("head", None, "seq"),
        P("seq"),
    )
    out_specs = P(None, ("seq", "head"), None)
    return jax.shard_map(
        on_device, mesh=mesh, in_specs=in_specs, out_specs=out_specs, check_vma=False
    )
```

```python
import math

import jax
import jax.numpy as jnp
from jax import lax
from jax.experimental import pallas as pl
from jax.experimental.pallas import tpu as pltpu
from jax.sharding import PartitionSpec as P

MESH = pl.DeviceIdType.MESH
SPAN = 768
XN, YLO, YHI, ZN = 4, 4, 2, 8
YN = YLO * YHI
HIGH, LOW = 8, 256
TILES = 8
F32, BF16 = jnp.float32, jnp.bfloat16


def nn(a, b):
    return lax.dot_general(a, b, (((1,), (0,)), ((), ())), preferred_element_type=F32)


def nt(a, b):
    return lax.dot_general(a, b, (((1,), (1,)), ((), ())), preferred_element_type=F32)


def split_halves(a, b):
    low = lax.broadcasted_iota(jnp.int32, a.shape, 1) < 4
    return (
        jnp.where(low, a, pltpu.roll(b, 4, 1)),
        jnp.where(low, pltpu.roll(a, 4, 1), b),
    )


def kernel(
    q_hbm, g_hbm, cb_hbm, ids_hbm, reach_hbm, out_ref,
    q_ref, g_ref, cb_ref, reach_ref, ids_all,
    cbt, onehot, high, rows, grads, low_ref, own_ref, part_ref, s_ref, d_ref, e_ref, w_ref,
    keep, csend, crecv, xsend, xrecv, yred, precv,
    in_s, id_s, id_r, c_s, c_r, x_s, x_r, line_s, p_s, p_r,
):
    tok = reach_ref.shape[1]
    words, width = cb_ref.shape[1], cb_ref.shape[2]
    n_rows = q_ref.shape[0]
    group = n_rows // tok
    blocks = SPAN // tok + 1
    scale = 1.0 / math.sqrt(width)
    seq, head = lax.axis_index("seq"), lax.axis_index("head")
    n_seq = lax.axis_size("seq")
    z = seq % ZN
    x = (seq // ZN) % XN
    x_hi, x_lo = x // 2, x % 2
    y_lo = seq // (ZN * XN)
    y_hi, core = head // 2, head % 2
    y = y_hi * YLO + y_lo

    def device(x_at, y_at, z_at, core_at):
        return (((y_at % YLO) * XN + x_at) * ZN + z_at, (y_at // YLO) * 2 + core_at)

    def x_other(j):
        hi = 1 - x_hi if j // 2 else x_hi
        lo = 1 - x_lo if j % 2 else x_lo
        return hi * 2 + lo

    buddy = device(x, y, z, 1 - core)
    x_peers = [device(x_other(j), y, z, core) for j in range(1, XN)]
    y_peers = [device(x, (y + i) % YN, z, core) for i in range(1, YN)]
    z_peers = [device(x, y, (z + i) % ZN, core) for i in range(1, ZN)]
    ahead = [((seq + i) % n_seq, head) for i in range(1, blocks)]
    behind = [((seq + n_seq - i) % n_seq, head) for i in range(1, blocks)]

    offsets = sorted(
        ((i, j) for i in range(YN) for j in range(ZN) if i or j),
        key=lambda at: -min(at[0], YN - at[0]) - min(at[1], ZN - at[1]),
    )

    barrier = pltpu.get_barrier_semaphore()
    greeted = behind + z_peers + y_peers + x_peers + [buddy]
    for peer in greeted:
        pl.semaphore_signal(barrier, inc=1, device_id=peer, device_id_type=MESH)

    loads = [
        pltpu.make_async_copy(src, dst, in_s.at[i])
        for i, (src, dst) in enumerate(
            (
                (ids_hbm, ids_all.at[blocks - 1]),
                (reach_hbm, reach_ref),
                (cb_hbm, cb_ref),
                (q_hbm, q_ref),
                (g_hbm, g_ref),
            )
        )
    ]
    for load in loads:
        load.start()
    grads[...] = jnp.zeros_like(grads)

    tile_tok = tok // TILES
    lanes = tile_tok * group
    tau = lax.broadcasted_iota(jnp.int32, (1, lanes), 1) // group
    at_tile = lax.broadcasted_iota(jnp.int32, (TILES, tok), 1) // tile_tok == lax.broadcasted_iota(
        jnp.int32, (TILES, tok), 0
    )
    spread = (
        lax.broadcasted_iota(jnp.int32, (tok, lanes), 0) % tile_tok
        == lax.broadcasted_iota(jnp.int32, (tok, lanes), 1) // group
    ).astype(F32).astype(BF16)

    def expand(part):
        return nn(jnp.where(at_tile, part.astype(F32), 0.0).astype(BF16), spread)

    loads[0].wait()
    loads[1].wait()
    place = seq * tok + lax.broadcasted_iota(jnp.int32, (1, tok), 1)
    reach = jnp.minimum(reach_ref[...], place + 1)
    reach_wide = (expand(reach // 256) * 256.0 + expand(reach % 256)).astype(jnp.int32)
    low_ref[...] = SPAN + tau - reach_wide

    loads[2].wait()
    for table in range(2):
        for h in range(HIGH):
            cbt[table, h * width : (h + 1) * width, :] = cb_ref[
                table, h * LOW : (h + 1) * LOW, :
            ].T

    pl.semaphore_wait(barrier, len(greeted))

    id_copies = []
    for i in range(blocks - 1):
        copy = pltpu.make_async_remote_copy(
            src_ref=ids_all.at[blocks - 1],
            dst_ref=ids_all.at[blocks - 2 - i],
            send_sem=id_s.at[i],
            recv_sem=id_r.at[i],
            device_id=ahead[i],
            device_id_type=MESH,
        )
        copy.start()
        id_copies.append(copy)

    for peer in y_peers:
        pl.semaphore_signal(line_s, inc=1, device_id=peer, device_id_type=MESH)

    def decode(block):
        cols = slice(block * tok, (block + 1) * tok)
        ids = ids_all[block]
        hi = ids // LOW
        columns = jnp.concatenate(
            [hi.astype(F32), jnp.zeros((6, tok), F32)], axis=0
        ).T
        word = lax.broadcasted_iota(jnp.int32, (LOW, tok), 0)
        for table in range(2):
            onehot[table, :, cols] = (
                (word == ids[table : table + 1, :] % LOW).astype(F32).astype(BF16)
            )
            high[table, cols, :] = jnp.broadcast_to(
                columns[:, table : table + 1], (tok, width)
            ).astype(BF16)
            found = nn(cbt[table], onehot[table, :, cols])
            own = found[:width]
            for h in range(1, HIGH):
                own = jnp.where(
                    hi[table : table + 1, :] == h, found[h * width : (h + 1) * width], own
                )
            rows[table, cols, :] = own.T.astype(BF16)

    win = SPAN + tile_tok
    step = tile_tok
    steps = win // step
    ramp = lax.broadcasted_iota(jnp.int32, (step, lanes), 0)
    inverse, shrink = {}, {}

    def queries_of(a):
        return slice(a * lanes, (a + 1) * lanes)

    def keys_of(a):
        return slice(a * tile_tok, a * tile_tok + win)

    def part_of(j):
        return slice(j * step, (j + 1) * step)

    exponent = scale * math.log2(math.e)

    def old_steps(a):
        return range(steps - 1 - a)

    def own_steps(a):
        return range(steps - 1 - a, steps)

    def masked_top(a, parts):
        low = low_ref[a : a + 1, :] - ramp
        top = None
        for j in parts:
            s = jnp.where(low < j * step, s_ref[a, part_of(j), :], -1e30)
            if j == steps - 1:
                s = jnp.where(ramp <= tau, s, -1e30)
            s_ref[a, part_of(j), :] = s
            top = s if top is None else jnp.maximum(top, s)
        return jnp.max(top, axis=0, keepdims=True)

    def exponentials(a, parts, top):
        norm = jnp.zeros((step, lanes), F32)
        for j in parts:
            p = jnp.exp2((s_ref[a, part_of(j), :] - top) * exponent)
            s_ref[a, part_of(j), :] = p
            norm = norm + p
        return jnp.sum(norm, axis=0, keepdims=True)

    def weighted_dots(a, parts):
        total = jnp.zeros((step, lanes), F32)
        for j in parts:
            total = total + s_ref[a, part_of(j), :] * d_ref[a, part_of(j), :]
        return jnp.sum(total, axis=0, keepdims=True)

    def own_part(a):
        top = masked_top(a, own_steps(a))
        own_ref[0, a : a + 1, :] = top
        own_ref[1, a : a + 1, :] = exponentials(a, own_steps(a), top)
        own_ref[2, a : a + 1, :] = weighted_dots(a, own_steps(a))

    def softmax(a):
        own_top = own_ref[0, a : a + 1, :]
        top = jnp.maximum(masked_top(a, old_steps(a)), own_top)
        shrink[a] = jnp.exp2((own_top - top) * exponent)
        norm = exponentials(a, old_steps(a), top) + own_ref[1, a : a + 1, :] * shrink[a]
        inverse[a] = 1.0 / norm
        for parts, factor in (
            (old_steps(a), inverse[a]),
            (own_steps(a), inverse[a] * shrink[a]),
        ):
            for j in parts:
                w_ref[a % 2, part_of(j), :] = (s_ref[a, part_of(j), :] * factor).astype(BF16)

    def score_gradient(a):
        total = weighted_dots(a, old_steps(a)) + own_ref[2, a : a + 1, :] * shrink[a]
        total = total * inverse[a]
        factor = inverse[a] * scale
        for parts, factor in ((old_steps(a), factor), (own_steps(a), factor * shrink[a])):
            for j in parts:
                p, d = s_ref[a, part_of(j), :], d_ref[a, part_of(j), :]
                e_ref[a % 2, part_of(j), :] = ((p * factor) * (d - total)).astype(BF16)

    def add_values(a):
        grads[1, keys_of(a), :] += nn(w_ref[a % 2], g_ref[queries_of(a), :])

    def add_keys(a):
        grads[0, keys_of(a), :] += nn(e_ref[a % 2], q_ref[queries_of(a), :])

    half = words // XN // 2
    y_rows = half // YLO
    c_copies, x_copies = {}, {}

    def scatter(table, flip):
        at_hi = 1 - x_hi if flip else x_hi
        part = grads[table].astype(BF16)
        wide = jnp.concatenate(
            [
                jnp.where(
                    high[table] == (at_y * 2 + at_hi).astype(F32).astype(BF16),
                    part,
                    jnp.zeros_like(part),
                )
                for at_y in range(YLO)
            ],
            axis=1,
        )
        part_ref[table] = nn(onehot[table], wide)

    def to_buddy(table, flip):
        for j in (flip * 2 + 1, flip * 2):
            at_lo = 1 - x_lo if j % 2 else x_lo
            span = pl.ds(pl.multiple_of(at_lo * (LOW // 2), LOW // 2), LOW // 2)
            for at_y in range(YLO):
                part = part_ref[table, span, at_y * width : (at_y + 1) * width]
                part = part.reshape(LOW // 32, 16, width)
                first, second = split_halves(part[:, :8, :], part[:, 8:, :])
                first, second = first.reshape(y_rows, width), second.reshape(y_rows, width)
                to = slice(at_y * y_rows, (at_y + 1) * y_rows)
                keep[table, j, to, :] = jnp.where(core == 0, first, second)
                csend[table, j, to, :] = jnp.where(core == 0, second, first).astype(BF16)
            copy = pltpu.make_async_remote_copy(
                src_ref=csend.at[table, j],
                dst_ref=crecv.at[table, j],
                send_sem=c_s.at[table, j],
                recv_sem=c_r.at[table, j],
                device_id=buddy,
                device_id_type=MESH,
            )
            copy.start()
            c_copies[table, j] = copy

    def to_x(table, j):
        c_copies[table, j].wait()
        xsend[table, j - 1] = (keep[table, j] + crecv[table, j].astype(F32)).astype(BF16)
        copy = pltpu.make_async_remote_copy(
            src_ref=xsend.at[table, j - 1],
            dst_ref=xrecv.at[table, j - 1],
            send_sem=x_s.at[table, j - 1],
            recv_sem=x_r.at[table, j - 1],
            device_id=x_peers[j - 1],
            device_id_type=MESH,
        )
        copy.start()
        x_copies[table, j] = copy

    def chip_line(table):
        c_copies[table, 0].wait()
        total = keep[table, 0] + crecv[table, 0].astype(F32)
        for j in (3, 2, 1):
            x_copies[table, j].wait()
            total = total + xrecv[table, j - 1].astype(F32)
        return total.reshape(half // 8, 8, width)

    decode(blocks - 1)
    for load in loads[3:]:
        load.wait()
    for a in range(TILES):
        own = slice(SPAN - a * step, win)
        own_keys = slice(SPAN, SPAN + (a + 1) * step)
        s_ref[a, own, :] = nt(rows[0, own_keys, :], q_ref[queries_of(a), :])
        d_ref[a, own, :] = nt(rows[1, own_keys, :], g_ref[queries_of(a), :])
        own_part(a)
    for i in range(blocks - 1):
        id_copies[i].wait()
        decode(blocks - 2 - i)

    for a in range(TILES):
        s_ref[a, : SPAN - a * step, :] = nt(
            rows[0, a * step : SPAN, :], q_ref[queries_of(a), :]
        )
        if a > 0:
            add_values(a - 1)
        softmax(a)
    add_values(TILES - 1)
    for flip in (1, 0):
        scatter(1, flip)
        to_buddy(1, flip)
    for a in range(TILES):
        d_ref[a, : SPAN - a * step, :] = nt(
            rows[1, a * step : SPAN, :], g_ref[queries_of(a), :]
        )
        if a > 0:
            add_keys(a - 1)
        if a == 3:
            for j in (3, 2, 1):
                to_x(1, j)
        score_gradient(a)
    add_keys(TILES - 1)
    scatter(0, 1)
    to_buddy(0, 1)
    scatter(0, 0)
    to_x(0, 3)
    to_x(0, 2)
    to_buddy(0, 0)
    to_x(0, 1)
    pl.semaphore_wait(line_s, len(y_peers))
    value_line = chip_line(1)
    key_line = chip_line(0)
    for at_hi, part in enumerate(split_halves(key_line, value_line)):
        yred[at_hi * YLO : (at_hi + 1) * YLO] = part.reshape(YLO, ZN, 8, width)
    for slot, (i, j) in enumerate(offsets):
        copy = pltpu.make_async_remote_copy(
            src_ref=yred.at[(y + i) % YN, (z + j) % ZN],
            dst_ref=precv.at[slot],
            send_sem=p_s,
            recv_sem=p_r,
            device_id=device(x, (y + i) % YN, (z + j) % ZN, core),
            device_id_type=MESH,
        )
        copy.start()
    pltpu.make_async_copy(precv, precv, p_r).wait()
    pltpu.make_async_copy(precv, precv, p_s).wait()
    done = yred[y, z] + jnp.sum(precv[...], axis=0)
    out_ref[...] = done


def on_device(queries, out_gradient, codebook, code_ids, reach_back):
    tok, heads, width = queries.shape
    words = codebook.shape[1]
    blocks = SPAN // tok + 1
    half = words // XN // 2
    dma = pltpu.SemaphoreType.DMA
    out = pl.pallas_call(
        kernel,
        out_shape=jax.ShapeDtypeStruct((8, width), F32),
        in_specs=[pl.BlockSpec(memory_space=pltpu.HBM)] * 5,
        out_specs=pl.BlockSpec(memory_space=pltpu.VMEM),
        scratch_shapes=[
            pltpu.VMEM((tok * heads, width), BF16),
            pltpu.VMEM((tok * heads, width), BF16),
            pltpu.VMEM((2, words, width), BF16),
            pltpu.VMEM((1, tok), jnp.int32),
            pltpu.VMEM((blocks, 2, tok), jnp.int32),
            pltpu.VMEM((2, HIGH * width, LOW), BF16),
            pltpu.VMEM((2, LOW, blocks * tok), BF16),
            pltpu.VMEM((2, blocks * tok, width), BF16),
            pltpu.VMEM((2, blocks * tok, width), BF16),
            pltpu.VMEM((2, blocks * tok, width), F32),
            pltpu.VMEM((TILES, tok), jnp.int32),
            pltpu.VMEM((3, TILES, tok), F32),
            pltpu.VMEM((2, LOW, YLO * width), F32),
            pltpu.VMEM((TILES, SPAN + tok // TILES, tok // TILES * heads), F32),
            pltpu.VMEM((TILES, SPAN + tok // TILES, tok // TILES * heads), F32),
            pltpu.VMEM((2, SPAN + tok // TILES, tok // TILES * heads), BF16),
            pltpu.VMEM((2, SPAN + tok // TILES, tok // TILES * heads), BF16),
            pltpu.VMEM((2, XN, half, width), F32),
            pltpu.VMEM((2, XN, half, width), BF16),
            pltpu.VMEM((2, XN, half, width), BF16),
            pltpu.VMEM((2, XN - 1, half, width), BF16),
            pltpu.VMEM((2, XN - 1, half, width), BF16),
            pltpu.VMEM((YN, ZN, 8, width), F32),
            pltpu.VMEM((YN * ZN - 1, 8, width), F32),
            dma((5,)),
            dma((blocks - 1,)), dma((blocks - 1,)),
            dma((2, XN)), dma((2, XN)),
            dma((2, XN - 1)), dma((2, XN - 1)),
            pltpu.SemaphoreType.REGULAR, dma, dma,
        ],
        compiler_params=pltpu.CompilerParams(
            collective_id=0, has_side_effects=True, vmem_limit_bytes=56 * 2**20
        ),
    )(
        queries.reshape(tok * heads, width),
        out_gradient.reshape(tok * heads, width),
        codebook,
        code_ids.reshape(2, tok),
        reach_back.reshape(1, tok),
    )
    return out.reshape(2, 4, width)


def solution(mesh):
    in_specs = (
        P("seq", "head", None),
        P("seq", "head", None),
        P(),
        P("head", None, "seq"),
        P("seq"),
    )
    out_specs = P(None, ("seq", "head"), None)
    return jax.shard_map(
        on_device, mesh=mesh, in_specs=in_specs, out_specs=out_specs, check_vma=False
    )
```

```python
import math

import jax
import jax.numpy as jnp
from jax import lax
from jax.experimental import pallas as pl
from jax.experimental.pallas import tpu as pltpu
from jax.sharding import PartitionSpec as P

MESH = pl.DeviceIdType.MESH
SPAN = 768
XN, YLO, YHI, ZN = 4, 4, 2, 8
YN = YLO * YHI
HIGH, LOW = 8, 256
TILES = 8
F32, BF16 = jnp.float32, jnp.bfloat16


def nn(a, b):
    return lax.dot_general(a, b, (((1,), (0,)), ((), ())), preferred_element_type=F32)


def nt(a, b):
    return lax.dot_general(a, b, (((1,), (1,)), ((), ())), preferred_element_type=F32)


def split_halves(a, b):
    low = lax.broadcasted_iota(jnp.int32, a.shape, 1) < 4
    return (
        jnp.where(low, a, pltpu.roll(b, 4, 1)),
        jnp.where(low, pltpu.roll(a, 4, 1), b),
    )


def kernel(
    q_hbm, g_hbm, cb_hbm, ids_hbm, reach_hbm, out_ref,
    q_ref, g_ref, cb_ref, reach_ref, ids_all,
    cbt, onehot, high, rows, grads, low_ref, own_ref, part_ref, s_ref, d_ref, e_ref, w_ref,
    keep, csend, crecv, xsend, xrecv, yred, ysend, precv,
    in_s, id_s, id_r, c_s, c_r, x_s, x_r, near_s, two_s, line_s, p_s, p_r,
):
    tok = reach_ref.shape[1]
    words, width = cb_ref.shape[1], cb_ref.shape[2]
    n_rows = q_ref.shape[0]
    group = n_rows // tok
    blocks = SPAN // tok + 1
    scale = 1.0 / math.sqrt(width)
    seq, head = lax.axis_index("seq"), lax.axis_index("head")
    n_seq = lax.axis_size("seq")
    z = seq % ZN
    x = (seq // ZN) % XN
    x_hi, x_lo = x // 2, x % 2
    y_lo = seq // (ZN * XN)
    y_hi, core = head // 2, head % 2
    y = y_hi * YLO + y_lo

    def device(x_at, y_at, z_at, core_at):
        return (((y_at % YLO) * XN + x_at) * ZN + z_at, (y_at // YLO) * 2 + core_at)

    def x_other(j):
        hi = 1 - x_hi if j // 2 else x_hi
        lo = 1 - x_lo if j % 2 else x_lo
        return hi * 2 + lo

    buddy = device(x, y, z, 1 - core)
    x_peers = [device(x_other(j), y, z, core) for j in range(1, XN)]
    y_peers = [device(x, (y + i) % YN, z, core) for i in range(1, YN)]

    def at_distance(i):
        return [
            device(x, (y + i) % YN, z, core),
            device(x, (y + YN - i) % YN, z, core),
            device(x, y, (z + i) % ZN, core),
            device(x, y, (z + ZN - i) % ZN, core),
        ]

    def tell(semaphore, peers):
        for peer in peers:
            pl.semaphore_signal(semaphore, inc=1, device_id=peer, device_id_type=MESH)

    ahead = [((seq + i) % n_seq, head) for i in range(1, blocks)]
    behind = [((seq + n_seq - i) % n_seq, head) for i in range(1, blocks)]

    offsets = sorted(
        ((i, j) for i in range(YN) for j in range(ZN) if i or j),
        key=lambda at: -min(at[0], YN - at[0]) - min(at[1], ZN - at[1]),
    )

    barrier = pltpu.get_barrier_semaphore()
    greeted = behind + at_distance(1) + x_peers + [buddy]
    for peer in greeted:
        pl.semaphore_signal(barrier, inc=1, device_id=peer, device_id_type=MESH)

    loads = [
        pltpu.make_async_copy(src, dst, in_s.at[i])
        for i, (src, dst) in enumerate(
            (
                (ids_hbm, ids_all.at[blocks - 1]),
                (reach_hbm, reach_ref),
                (cb_hbm, cb_ref),
                (q_hbm, q_ref),
                (g_hbm, g_ref),
            )
        )
    ]
    for load in loads:
        load.start()
    grads[...] = jnp.zeros_like(grads)

    tile_tok = tok // TILES
    lanes = tile_tok * group
    tau = lax.broadcasted_iota(jnp.int32, (1, lanes), 1) // group
    at_tile = lax.broadcasted_iota(jnp.int32, (TILES, tok), 1) // tile_tok == lax.broadcasted_iota(
        jnp.int32, (TILES, tok), 0
    )
    spread = (
        lax.broadcasted_iota(jnp.int32, (tok, lanes), 0) % tile_tok
        == lax.broadcasted_iota(jnp.int32, (tok, lanes), 1) // group
    ).astype(F32).astype(BF16)

    def expand(part):
        return nn(jnp.where(at_tile, part.astype(F32), 0.0).astype(BF16), spread)

    loads[0].wait()
    loads[1].wait()
    place = seq * tok + lax.broadcasted_iota(jnp.int32, (1, tok), 1)
    reach = jnp.minimum(reach_ref[...], place + 1)
    reach_wide = (expand(reach // 256) * 256.0 + expand(reach % 256)).astype(jnp.int32)
    low_ref[...] = SPAN + tau - reach_wide

    loads[2].wait()
    for table in range(2):
        for h in range(HIGH):
            cbt[table, h * width : (h + 1) * width, :] = cb_ref[
                table, h * LOW : (h + 1) * LOW, :
            ].T

    pl.semaphore_wait(barrier, len(greeted))

    id_copies = []
    for i in range(blocks - 1):
        copy = pltpu.make_async_remote_copy(
            src_ref=ids_all.at[blocks - 1],
            dst_ref=ids_all.at[blocks - 2 - i],
            send_sem=id_s.at[i],
            recv_sem=id_r.at[i],
            device_id=ahead[i],
            device_id_type=MESH,
        )
        copy.start()
        id_copies.append(copy)

    tell(near_s, at_distance(1))

    def decode(block):
        cols = slice(block * tok, (block + 1) * tok)
        ids = ids_all[block]
        hi = ids // LOW
        columns = jnp.concatenate(
            [hi.astype(F32), jnp.zeros((6, tok), F32)], axis=0
        ).T
        word = lax.broadcasted_iota(jnp.int32, (LOW, tok), 0)
        for table in range(2):
            onehot[table, :, cols] = (
                (word == ids[table : table + 1, :] % LOW).astype(F32).astype(BF16)
            )
            high[table, cols, :] = jnp.broadcast_to(
                columns[:, table : table + 1], (tok, width)
            ).astype(BF16)
            found = nn(cbt[table], onehot[table, :, cols])
            own = found[:width]
            for h in range(1, HIGH):
                own = jnp.where(
                    hi[table : table + 1, :] == h, found[h * width : (h + 1) * width], own
                )
            rows[table, cols, :] = own.T.astype(BF16)

    win = SPAN + tile_tok
    step = tile_tok
    steps = win // step
    ramp = lax.broadcasted_iota(jnp.int32, (step, lanes), 0)
    inverse, shrink = {}, {}

    def queries_of(a):
        return slice(a * lanes, (a + 1) * lanes)

    def keys_of(a):
        return slice(a * tile_tok, a * tile_tok + win)

    def part_of(j):
        return slice(j * step, (j + 1) * step)

    exponent = scale * math.log2(math.e)

    def old_steps(a):
        return range(steps - 1 - a)

    def own_steps(a):
        return range(steps - 1 - a, steps)

    def masked_top(a, parts):
        low = low_ref[a : a + 1, :] - ramp
        top = None
        for j in parts:
            s = jnp.where(low < j * step, s_ref[a, part_of(j), :], -1e30)
            if j == steps - 1:
                s = jnp.where(ramp <= tau, s, -1e30)
            s_ref[a, part_of(j), :] = s
            top = s if top is None else jnp.maximum(top, s)
        return jnp.max(top, axis=0, keepdims=True)

    def exponentials(a, parts, top):
        norm = jnp.zeros((step, lanes), F32)
        for j in parts:
            p = jnp.exp2((s_ref[a, part_of(j), :] - top) * exponent)
            s_ref[a, part_of(j), :] = p
            norm = norm + p
        return jnp.sum(norm, axis=0, keepdims=True)

    def weighted_dots(a, parts):
        total = jnp.zeros((step, lanes), F32)
        for j in parts:
            total = total + s_ref[a, part_of(j), :] * d_ref[a, part_of(j), :]
        return jnp.sum(total, axis=0, keepdims=True)

    def own_part(a):
        top = masked_top(a, own_steps(a))
        own_ref[0, a : a + 1, :] = top
        own_ref[1, a : a + 1, :] = exponentials(a, own_steps(a), top)
        own_ref[2, a : a + 1, :] = weighted_dots(a, own_steps(a))

    def softmax(a):
        own_top = own_ref[0, a : a + 1, :]
        top = jnp.maximum(masked_top(a, old_steps(a)), own_top)
        shrink[a] = jnp.exp2((own_top - top) * exponent)
        norm = exponentials(a, old_steps(a), top) + own_ref[1, a : a + 1, :] * shrink[a]
        inverse[a] = 1.0 / norm
        for parts, factor in (
            (old_steps(a), inverse[a]),
            (own_steps(a), inverse[a] * shrink[a]),
        ):
            for j in parts:
                w_ref[a % 2, part_of(j), :] = (s_ref[a, part_of(j), :] * factor).astype(BF16)

    def score_gradient(a):
        total = weighted_dots(a, old_steps(a)) + own_ref[2, a : a + 1, :] * shrink[a]
        total = total * inverse[a]
        factor = inverse[a] * scale
        for parts, factor in ((old_steps(a), factor), (own_steps(a), factor * shrink[a])):
            for j in parts:
                p, d = s_ref[a, part_of(j), :], d_ref[a, part_of(j), :]
                e_ref[a % 2, part_of(j), :] = ((p * factor) * (d - total)).astype(BF16)

    def add_values(a):
        grads[1, keys_of(a), :] += nn(w_ref[a % 2], g_ref[queries_of(a), :])

    def add_keys(a):
        grads[0, keys_of(a), :] += nn(e_ref[a % 2], q_ref[queries_of(a), :])

    half = words // XN // 2
    y_rows = half // YLO
    c_copies, x_copies = {}, {}

    def scatter(table, flip):
        at_hi = 1 - x_hi if flip else x_hi
        part = grads[table].astype(BF16)
        wide = jnp.concatenate(
            [
                jnp.where(
                    high[table] == (at_y * 2 + at_hi).astype(F32).astype(BF16),
                    part,
                    jnp.zeros_like(part),
                )
                for at_y in range(YLO)
            ],
            axis=1,
        )
        part_ref[table] = nn(onehot[table], wide)

    def to_buddy(table, flip):
        for j in (flip * 2 + 1, flip * 2):
            at_lo = 1 - x_lo if j % 2 else x_lo
            span = pl.ds(pl.multiple_of(at_lo * (LOW // 2), LOW // 2), LOW // 2)
            for at_y in range(YLO):
                part = part_ref[table, span, at_y * width : (at_y + 1) * width]
                part = part.reshape(LOW // 32, 16, width)
                first, second = split_halves(part[:, :8, :], part[:, 8:, :])
                first, second = first.reshape(y_rows, width), second.reshape(y_rows, width)
                to = slice(at_y * y_rows, (at_y + 1) * y_rows)
                keep[table, j, to, :] = jnp.where(core == 0, first, second)
                csend[table, j, to, :] = jnp.where(core == 0, second, first).astype(BF16)
            copy = pltpu.make_async_remote_copy(
                src_ref=csend.at[table, j],
                dst_ref=crecv.at[table, j],
                send_sem=c_s.at[table, j],
                recv_sem=c_r.at[table, j],
                device_id=buddy,
                device_id_type=MESH,
            )
            copy.start()
            c_copies[table, j] = copy

    def to_x(table, j):
        c_copies[table, j].wait()
        xsend[table, j - 1] = (keep[table, j] + crecv[table, j].astype(F32)).astype(BF16)
        copy = pltpu.make_async_remote_copy(
            src_ref=xsend.at[table, j - 1],
            dst_ref=xrecv.at[table, j - 1],
            send_sem=x_s.at[table, j - 1],
            recv_sem=x_r.at[table, j - 1],
            device_id=x_peers[j - 1],
            device_id_type=MESH,
        )
        copy.start()
        x_copies[table, j] = copy

    def chip_line(table):
        c_copies[table, 0].wait()
        total = keep[table, 0] + crecv[table, 0].astype(F32)
        for j in (3, 2, 1):
            x_copies[table, j].wait()
            total = total + xrecv[table, j - 1].astype(F32)
        return total.reshape(half // 8, 8, width)

    decode(blocks - 1)
    for load in loads[3:]:
        load.wait()
    for a in range(TILES):
        own = slice(SPAN - a * step, win)
        own_keys = slice(SPAN, SPAN + (a + 1) * step)
        s_ref[a, own, :] = nt(rows[0, own_keys, :], q_ref[queries_of(a), :])
        d_ref[a, own, :] = nt(rows[1, own_keys, :], g_ref[queries_of(a), :])
        own_part(a)
    for i in range(blocks - 1):
        id_copies[i].wait()
        decode(blocks - 2 - i)
    pl.semaphore_wait(near_s, 4)
    tell(two_s, at_distance(2))

    for a in range(TILES):
        s_ref[a, : SPAN - a * step, :] = nt(
            rows[0, a * step : SPAN, :], q_ref[queries_of(a), :]
        )
        if a > 0:
            add_values(a - 1)
        softmax(a)
    add_values(TILES - 1)
    pl.semaphore_wait(two_s, 4)
    tell(line_s, y_peers)
    for flip in (1, 0):
        scatter(1, flip)
        to_buddy(1, flip)
    for a in range(TILES):
        d_ref[a, : SPAN - a * step, :] = nt(
            rows[1, a * step : SPAN, :], g_ref[queries_of(a), :]
        )
        if a > 0:
            add_keys(a - 1)
        if a == 2:
            for j in (3, 2, 1):
                to_x(1, j)
        score_gradient(a)
    add_keys(TILES - 1)
    scatter(0, 1)
    to_buddy(0, 1)
    scatter(0, 0)
    to_x(0, 3)
    to_x(0, 2)
    to_buddy(0, 0)
    to_x(0, 1)
    pl.semaphore_wait(line_s, len(y_peers))
    value_line = chip_line(1)
    key_line = chip_line(0)
    for at_hi, part in enumerate(split_halves(key_line, value_line)):
        yred[at_hi * YLO : (at_hi + 1) * YLO] = part.reshape(YLO, ZN, 8, width)
    ysend[...] = yred[...].astype(BF16)
    for slot, (i, j) in enumerate(offsets):
        copy = pltpu.make_async_remote_copy(
            src_ref=ysend.at[(y + i) % YN, (z + j) % ZN],
            dst_ref=precv.at[slot],
            send_sem=p_s,
            recv_sem=p_r,
            device_id=device(x, (y + i) % YN, (z + j) % ZN, core),
            device_id_type=MESH,
        )
        copy.start()
    pltpu.make_async_copy(precv, precv, p_r).wait()
    pltpu.make_async_copy(precv, precv, p_s).wait()
    done = yred[y, z] + jnp.sum(precv[...].astype(F32), axis=0)
    out_ref[...] = done


def on_device(queries, out_gradient, codebook, code_ids, reach_back):
    tok, heads, width = queries.shape
    words = codebook.shape[1]
    blocks = SPAN // tok + 1
    half = words // XN // 2
    dma = pltpu.SemaphoreType.DMA
    out = pl.pallas_call(
        kernel,
        out_shape=jax.ShapeDtypeStruct((8, width), F32),
        in_specs=[pl.BlockSpec(memory_space=pltpu.HBM)] * 5,
        out_specs=pl.BlockSpec(memory_space=pltpu.VMEM),
        scratch_shapes=[
            pltpu.VMEM((tok * heads, width), BF16),
            pltpu.VMEM((tok * heads, width), BF16),
            pltpu.VMEM((2, words, width), BF16),
            pltpu.VMEM((1, tok), jnp.int32),
            pltpu.VMEM((blocks, 2, tok), jnp.int32),
            pltpu.VMEM((2, HIGH * width, LOW), BF16),
            pltpu.VMEM((2, LOW, blocks * tok), BF16),
            pltpu.VMEM((2, blocks * tok, width), BF16),
            pltpu.VMEM((2, blocks * tok, width), BF16),
            pltpu.VMEM((2, blocks * tok, width), F32),
            pltpu.VMEM((TILES, tok), jnp.int32),
            pltpu.VMEM((3, TILES, tok), F32),
            pltpu.VMEM((2, LOW, YLO * width), F32),
            pltpu.VMEM((TILES, SPAN + tok // TILES, tok // TILES * heads), F32),
            pltpu.VMEM((TILES, SPAN + tok // TILES, tok // TILES * heads), F32),
            pltpu.VMEM((2, SPAN + tok // TILES, tok // TILES * heads), BF16),
            pltpu.VMEM((2, SPAN + tok // TILES, tok // TILES * heads), BF16),
            pltpu.VMEM((2, XN, half, width), F32),
            pltpu.VMEM((2, XN, half, width), BF16),
            pltpu.VMEM((2, XN, half, width), BF16),
            pltpu.VMEM((2, XN - 1, half, width), BF16),
            pltpu.VMEM((2, XN - 1, half, width), BF16),
            pltpu.VMEM((YN, ZN, 8, width), F32),
            pltpu.VMEM((YN, ZN, 8, width), BF16),
            pltpu.VMEM((YN * ZN - 1, 8, width), BF16),
            dma((5,)),
            dma((blocks - 1,)), dma((blocks - 1,)),
            dma((2, XN)), dma((2, XN)),
            dma((2, XN - 1)), dma((2, XN - 1)),
            *[pltpu.SemaphoreType.REGULAR] * 3, dma, dma,
        ],
        compiler_params=pltpu.CompilerParams(
            collective_id=0, has_side_effects=True, vmem_limit_bytes=56 * 2**20
        ),
    )(
        queries.reshape(tok * heads, width),
        out_gradient.reshape(tok * heads, width),
        codebook,
        code_ids.reshape(2, tok),
        reach_back.reshape(1, tok),
    )
    return out.reshape(2, 4, width)


def solution(mesh):
    in_specs = (
        P("seq", "head", None),
        P("seq", "head", None),
        P(),
        P("head", None, "seq"),
        P("seq"),
    )
    out_specs = P(None, ("seq", "head"), None)
    return jax.shard_map(
        on_device, mesh=mesh, in_specs=in_specs, out_specs=out_specs, check_vma=False
    )
```

```python
import math

import jax
import jax.numpy as jnp
from jax import lax
from jax.experimental import pallas as pl
from jax.experimental.pallas import tpu as pltpu
from jax.sharding import PartitionSpec as P

MESH = pl.DeviceIdType.MESH
SPAN = 768
XN, YLO, YHI, ZN = 4, 4, 2, 8
YN = YLO * YHI
HIGH, LOW = 8, 256
TILES = 8
F32, BF16 = jnp.float32, jnp.bfloat16


def nn(a, b):
    return lax.dot_general(a, b, (((1,), (0,)), ((), ())), preferred_element_type=F32)


def nt(a, b):
    return lax.dot_general(a, b, (((1,), (1,)), ((), ())), preferred_element_type=F32)


def split_halves(a, b):
    low = lax.broadcasted_iota(jnp.int32, a.shape, 1) < 4
    return (
        jnp.where(low, a, pltpu.roll(b, 4, 1)),
        jnp.where(low, pltpu.roll(a, 4, 1), b),
    )


def kernel(
    q_hbm, g_hbm, cb_hbm, ids_hbm, reach_hbm, out_ref,
    q_ref, g_ref, cb_ref, reach_ref, ids_all,
    cbt, onehot, high, rows, grads, low_ref, own_ref, part_ref, s_ref, d_ref, e_ref, w_ref,
    keep, csend, crecv, xsend, xrecv, yred, ysend, precv,
    in_s, id_s, id_r, c_s, c_r, x_s, x_r, near_s, two_s, line_s, p_s, p_r,
):
    tok = reach_ref.shape[1]
    words, width = cb_ref.shape[1], cb_ref.shape[2]
    n_rows = q_ref.shape[0]
    group = n_rows // tok
    blocks = SPAN // tok + 1
    scale = 1.0 / math.sqrt(width)
    seq, head = lax.axis_index("seq"), lax.axis_index("head")
    n_seq = lax.axis_size("seq")
    z = seq % ZN
    x = (seq // ZN) % XN
    x_hi, x_lo = x // 2, x % 2
    y_lo = seq // (ZN * XN)
    y_hi, core = head // 2, head % 2
    y = y_hi * YLO + y_lo

    def device(x_at, y_at, z_at, core_at):
        return (((y_at % YLO) * XN + x_at) * ZN + z_at, (y_at // YLO) * 2 + core_at)

    def x_other(j):
        hi = 1 - x_hi if j // 2 else x_hi
        lo = 1 - x_lo if j % 2 else x_lo
        return hi * 2 + lo

    buddy = device(x, y, z, 1 - core)
    x_peers = [device(x_other(j), y, z, core) for j in range(1, XN)]
    y_peers = [device(x, (y + i) % YN, z, core) for i in range(1, YN)]

    def at_distance(i):
        return [
            device(x, (y + i) % YN, z, core),
            device(x, (y + YN - i) % YN, z, core),
            device(x, y, (z + i) % ZN, core),
            device(x, y, (z + ZN - i) % ZN, core),
        ]

    def tell(semaphore, peers):
        for peer in peers:
            pl.semaphore_signal(semaphore, inc=1, device_id=peer, device_id_type=MESH)

    ahead = [((seq + i) % n_seq, head) for i in range(1, blocks)]
    behind = [((seq + n_seq - i) % n_seq, head) for i in range(1, blocks)]

    offsets = sorted(
        ((i, j) for i in range(YN) for j in range(ZN) if i or j),
        key=lambda at: -min(at[0], YN - at[0]) - min(at[1], ZN - at[1]),
    )

    barrier = pltpu.get_barrier_semaphore()
    greeted = behind + at_distance(1) + x_peers + [buddy]
    for peer in greeted:
        pl.semaphore_signal(barrier, inc=1, device_id=peer, device_id_type=MESH)

    loads = [
        pltpu.make_async_copy(src, dst, in_s.at[i])
        for i, (src, dst) in enumerate(
            (
                (ids_hbm, ids_all.at[blocks - 1]),
                (reach_hbm, reach_ref),
                (cb_hbm, cb_ref),
                (q_hbm, q_ref),
                (g_hbm, g_ref),
            )
        )
    ]
    for load in loads:
        load.start()
    loads[0].wait()
    pl.semaphore_wait(barrier, len(greeted))

    id_copies = []
    for i in range(blocks - 1):
        copy = pltpu.make_async_remote_copy(
            src_ref=ids_all.at[blocks - 1],
            dst_ref=ids_all.at[blocks - 2 - i],
            send_sem=id_s.at[i],
            recv_sem=id_r.at[i],
            device_id=ahead[i],
            device_id_type=MESH,
        )
        copy.start()
        id_copies.append(copy)

    tell(near_s, at_distance(1))

    grads[...] = jnp.zeros_like(grads)

    tile_tok = tok // TILES
    lanes = tile_tok * group
    tau = lax.broadcasted_iota(jnp.int32, (1, lanes), 1) // group
    at_tile = lax.broadcasted_iota(jnp.int32, (TILES, tok), 1) // tile_tok == lax.broadcasted_iota(
        jnp.int32, (TILES, tok), 0
    )
    spread = (
        lax.broadcasted_iota(jnp.int32, (tok, lanes), 0) % tile_tok
        == lax.broadcasted_iota(jnp.int32, (tok, lanes), 1) // group
    ).astype(F32).astype(BF16)

    def expand(part):
        return nn(jnp.where(at_tile, part.astype(F32), 0.0).astype(BF16), spread)

    loads[1].wait()
    place = seq * tok + lax.broadcasted_iota(jnp.int32, (1, tok), 1)
    reach = jnp.minimum(reach_ref[...], place + 1)
    reach_wide = (expand(reach // 256) * 256.0 + expand(reach % 256)).astype(jnp.int32)
    low_ref[...] = SPAN + tau - reach_wide

    loads[2].wait()
    for table in range(2):
        for h in range(HIGH):
            cbt[table, h * width : (h + 1) * width, :] = cb_ref[
                table, h * LOW : (h + 1) * LOW, :
            ].T

    def decode(block):
        cols = slice(block * tok, (block + 1) * tok)
        ids = ids_all[block]
        hi = ids // LOW
        columns = jnp.concatenate(
            [hi.astype(F32), jnp.zeros((6, tok), F32)], axis=0
        ).T
        word = lax.broadcasted_iota(jnp.int32, (LOW, tok), 0)
        for table in range(2):
            onehot[table, :, cols] = (
                (word == ids[table : table + 1, :] % LOW).astype(F32).astype(BF16)
            )
            high[table, cols, :] = jnp.broadcast_to(
                columns[:, table : table + 1], (tok, width)
            ).astype(BF16)
            found = nn(cbt[table], onehot[table, :, cols])
            own = found[:width]
            for h in range(1, HIGH):
                own = jnp.where(
                    hi[table : table + 1, :] == h, found[h * width : (h + 1) * width], own
                )
            rows[table, cols, :] = own.T.astype(BF16)

    win = SPAN + tile_tok
    step = tile_tok
    steps = win // step
    ramp = lax.broadcasted_iota(jnp.int32, (step, lanes), 0)
    inverse, shrink = {}, {}

    def queries_of(a):
        return slice(a * lanes, (a + 1) * lanes)

    def keys_of(a):
        return slice(a * tile_tok, a * tile_tok + win)

    def part_of(j):
        return slice(j * step, (j + 1) * step)

    exponent = scale * math.log2(math.e)

    def old_steps(a):
        return range(steps - 1 - a)

    def own_steps(a):
        return range(steps - 1 - a, steps)

    def masked_top(a, parts):
        low = low_ref[a : a + 1, :] - ramp
        top = None
        for j in parts:
            s = jnp.where(low < j * step, s_ref[a, part_of(j), :], -1e30)
            if j == steps - 1:
                s = jnp.where(ramp <= tau, s, -1e30)
            s_ref[a, part_of(j), :] = s
            top = s if top is None else jnp.maximum(top, s)
        return jnp.max(top, axis=0, keepdims=True)

    def exponentials(a, parts, top):
        norm = jnp.zeros((step, lanes), F32)
        for j in parts:
            p = jnp.exp2((s_ref[a, part_of(j), :] - top) * exponent)
            s_ref[a, part_of(j), :] = p
            norm = norm + p
        return jnp.sum(norm, axis=0, keepdims=True)

    def weighted_dots(a, parts):
        total = jnp.zeros((step, lanes), F32)
        for j in parts:
            total = total + s_ref[a, part_of(j), :] * d_ref[a, part_of(j), :]
        return jnp.sum(total, axis=0, keepdims=True)

    def own_part(a):
        top = masked_top(a, own_steps(a))
        own_ref[0, a : a + 1, :] = top
        own_ref[1, a : a + 1, :] = exponentials(a, own_steps(a), top)
        own_ref[2, a : a + 1, :] = weighted_dots(a, own_steps(a))

    def softmax(a):
        own_top = own_ref[0, a : a + 1, :]
        top = jnp.maximum(masked_top(a, old_steps(a)), own_top)
        shrink[a] = jnp.exp2((own_top - top) * exponent)
        norm = exponentials(a, old_steps(a), top) + own_ref[1, a : a + 1, :] * shrink[a]
        inverse[a] = 1.0 / norm
        for parts, factor in (
            (old_steps(a), inverse[a]),
            (own_steps(a), inverse[a] * shrink[a]),
        ):
            for j in parts:
                w_ref[a % 2, part_of(j), :] = (s_ref[a, part_of(j), :] * factor).astype(BF16)

    def score_gradient(a):
        total = weighted_dots(a, old_steps(a)) + own_ref[2, a : a + 1, :] * shrink[a]
        total = total * inverse[a]
        factor = inverse[a] * scale
        for parts, factor in ((old_steps(a), factor), (own_steps(a), factor * shrink[a])):
            for j in parts:
                p, d = s_ref[a, part_of(j), :], d_ref[a, part_of(j), :]
                e_ref[a % 2, part_of(j), :] = ((p * factor) * (d - total)).astype(BF16)

    def add_values(a):
        grads[1, keys_of(a), :] += nn(w_ref[a % 2], g_ref[queries_of(a), :])

    def add_keys(a):
        grads[0, keys_of(a), :] += nn(e_ref[a % 2], q_ref[queries_of(a), :])

    half = words // XN // 2
    y_rows = half // YLO
    c_copies, x_copies = {}, {}

    def scatter(table, flip):
        at_hi = 1 - x_hi if flip else x_hi
        part = grads[table].astype(BF16)
        wide = jnp.concatenate(
            [
                jnp.where(
                    high[table] == (at_y * 2 + at_hi).astype(F32).astype(BF16),
                    part,
                    jnp.zeros_like(part),
                )
                for at_y in range(YLO)
            ],
            axis=1,
        )
        part_ref[table] = nn(onehot[table], wide)

    def to_buddy(table, flip):
        for j in (flip * 2 + 1, flip * 2):
            at_lo = 1 - x_lo if j % 2 else x_lo
            span = pl.ds(pl.multiple_of(at_lo * (LOW // 2), LOW // 2), LOW // 2)
            for at_y in range(YLO):
                part = part_ref[table, span, at_y * width : (at_y + 1) * width]
                part = part.reshape(LOW // 32, 16, width)
                first, second = split_halves(part[:, :8, :], part[:, 8:, :])
                first, second = first.reshape(y_rows, width), second.reshape(y_rows, width)
                to = slice(at_y * y_rows, (at_y + 1) * y_rows)
                keep[table, j, to, :] = jnp.where(core == 0, first, second)
                csend[table, j, to, :] = jnp.where(core == 0, second, first).astype(BF16)
            copy = pltpu.make_async_remote_copy(
                src_ref=csend.at[table, j],
                dst_ref=crecv.at[table, j],
                send_sem=c_s.at[table, j],
                recv_sem=c_r.at[table, j],
                device_id=buddy,
                device_id_type=MESH,
            )
            copy.start()
            c_copies[table, j] = copy

    def to_x(table, j):
        c_copies[table, j].wait()
        xsend[table, j - 1] = (keep[table, j] + crecv[table, j].astype(F32)).astype(BF16)
        copy = pltpu.make_async_remote_copy(
            src_ref=xsend.at[table, j - 1],
            dst_ref=xrecv.at[table, j - 1],
            send_sem=x_s.at[table, j - 1],
            recv_sem=x_r.at[table, j - 1],
            device_id=x_peers[j - 1],
            device_id_type=MESH,
        )
        copy.start()
        x_copies[table, j] = copy

    def chip_line(table):
        c_copies[table, 0].wait()
        total = keep[table, 0] + crecv[table, 0].astype(F32)
        for j in (3, 2, 1):
            x_copies[table, j].wait()
            total = total + xrecv[table, j - 1].astype(F32)
        return total.reshape(half // 8, 8, width)

    decode(blocks - 1)
    for load in loads[3:]:
        load.wait()
    for a in range(TILES):
        own = slice(SPAN - a * step, win)
        own_keys = slice(SPAN, SPAN + (a + 1) * step)
        s_ref[a, own, :] = nt(rows[0, own_keys, :], q_ref[queries_of(a), :])
        d_ref[a, own, :] = nt(rows[1, own_keys, :], g_ref[queries_of(a), :])
        own_part(a)
    pl.semaphore_wait(near_s, 4)
    tell(two_s, at_distance(2))
    for i in range(blocks - 1):
        id_copies[i].wait()
        decode(blocks - 2 - i)

    def old_scores(a):
        s_ref[a, : SPAN - a * step, :] = nt(
            rows[0, a * step : SPAN, :], q_ref[queries_of(a), :]
        )

    def old_dots(a):
        d_ref[a, : SPAN - a * step, :] = nt(
            rows[1, a * step : SPAN, :], g_ref[queries_of(a), :]
        )

    old_scores(0)
    for a in range(TILES):
        if a < TILES - 1:
            old_scores(a + 1)
        if a > 0:
            add_values(a - 1)
        softmax(a)
    add_values(TILES - 1)
    pl.semaphore_wait(two_s, 4)
    tell(line_s, y_peers)
    old_dots(0)
    for flip in (1, 0):
        scatter(1, flip)
        to_buddy(1, flip)
    for a in range(TILES):
        if a < TILES - 1:
            old_dots(a + 1)
        if a > 0:
            add_keys(a - 1)
        if a == 2:
            for j in (3, 2, 1):
                to_x(1, j)
        score_gradient(a)
    add_keys(TILES - 1)
    scatter(0, 1)
    to_buddy(0, 1)
    scatter(0, 0)
    to_x(0, 3)
    to_x(0, 2)
    to_buddy(0, 0)
    to_x(0, 1)
    pl.semaphore_wait(line_s, len(y_peers))
    value_line = chip_line(1)
    key_line = chip_line(0)
    for at_hi, part in enumerate(split_halves(key_line, value_line)):
        yred[at_hi * YLO : (at_hi + 1) * YLO] = part.reshape(YLO, ZN, 8, width)
    ysend[...] = yred[...].astype(BF16)
    for slot, (i, j) in enumerate(offsets):
        copy = pltpu.make_async_remote_copy(
            src_ref=ysend.at[(y + i) % YN, (z + j) % ZN],
            dst_ref=precv.at[slot],
            send_sem=p_s,
            recv_sem=p_r,
            device_id=device(x, (y + i) % YN, (z + j) % ZN, core),
            device_id_type=MESH,
        )
        copy.start()
    pltpu.make_async_copy(precv, precv, p_r).wait()
    pltpu.make_async_copy(precv, precv, p_s).wait()
    done = yred[y, z] + jnp.sum(precv[...].astype(F32), axis=0)
    out_ref[...] = done


def on_device(queries, out_gradient, codebook, code_ids, reach_back):
    tok, heads, width = queries.shape
    words = codebook.shape[1]
    blocks = SPAN // tok + 1
    half = words // XN // 2
    dma = pltpu.SemaphoreType.DMA
    out = pl.pallas_call(
        kernel,
        out_shape=jax.ShapeDtypeStruct((8, width), F32),
        in_specs=[pl.BlockSpec(memory_space=pltpu.HBM)] * 5,
        out_specs=pl.BlockSpec(memory_space=pltpu.VMEM),
        scratch_shapes=[
            pltpu.VMEM((tok * heads, width), BF16),
            pltpu.VMEM((tok * heads, width), BF16),
            pltpu.VMEM((2, words, width), BF16),
            pltpu.VMEM((1, tok), jnp.int32),
            pltpu.VMEM((blocks, 2, tok), jnp.int32),
            pltpu.VMEM((2, HIGH * width, LOW), BF16),
            pltpu.VMEM((2, LOW, blocks * tok), BF16),
            pltpu.VMEM((2, blocks * tok, width), BF16),
            pltpu.VMEM((2, blocks * tok, width), BF16),
            pltpu.VMEM((2, blocks * tok, width), F32),
            pltpu.VMEM((TILES, tok), jnp.int32),
            pltpu.VMEM((3, TILES, tok), F32),
            pltpu.VMEM((2, LOW, YLO * width), F32),
            pltpu.VMEM((TILES, SPAN + tok // TILES, tok // TILES * heads), F32),
            pltpu.VMEM((TILES, SPAN + tok // TILES, tok // TILES * heads), F32),
            pltpu.VMEM((2, SPAN + tok // TILES, tok // TILES * heads), BF16),
            pltpu.VMEM((2, SPAN + tok // TILES, tok // TILES * heads), BF16),
            pltpu.VMEM((2, XN, half, width), F32),
            pltpu.VMEM((2, XN, half, width), BF16),
            pltpu.VMEM((2, XN, half, width), BF16),
            pltpu.VMEM((2, XN - 1, half, width), BF16),
            pltpu.VMEM((2, XN - 1, half, width), BF16),
            pltpu.VMEM((YN, ZN, 8, width), F32),
            pltpu.VMEM((YN, ZN, 8, width), BF16),
            pltpu.VMEM((YN * ZN - 1, 8, width), BF16),
            dma((5,)),
            dma((blocks - 1,)), dma((blocks - 1,)),
            dma((2, XN)), dma((2, XN)),
            dma((2, XN - 1)), dma((2, XN - 1)),
            *[pltpu.SemaphoreType.REGULAR] * 3, dma, dma,
        ],
        compiler_params=pltpu.CompilerParams(
            collective_id=0, has_side_effects=True, vmem_limit_bytes=56 * 2**20
        ),
    )(
        queries.reshape(tok * heads, width),
        out_gradient.reshape(tok * heads, width),
        codebook,
        code_ids.reshape(2, tok),
        reach_back.reshape(1, tok),
    )
    return out.reshape(2, 4, width)


def solution(mesh):
    in_specs = (
        P("seq", "head", None),
        P("seq", "head", None),
        P(),
        P("head", None, "seq"),
        P("seq"),
    )
    out_specs = P(None, ("seq", "head"), None)
    return jax.shard_map(
        on_device, mesh=mesh, in_specs=in_specs, out_specs=out_specs, check_vma=False
    )
```
